256 devices in a mesh: tm: 8 (over y, core), pencil: 32 (over z, x).
Axes of the slice: x: 4, y: 4, z: 8, core: 2. Of those that a mesh axis runs over, the one named last changes fastest.
Arguments:
- initial: float32 [128, 64, 128], P('pencil'), may hold values from -6 to 6
- conductivity: float32 [128, 64, 128], P('pencil'), may hold values from 0.25 to 4
- source: float32 [128, 64, 128], P('pencil'), may hold values from -2 to 2.7
Outputs:
- final_states: float32 [8, 128, 64, 128], P('tm', 'pencil')
The draws below stay inside these ranges and needn't reach their ends.
All inputs are finite; a program needn't handle non-finite values.
Results may differ from the reference program's by a relative error of at most 0.0002.
Values sent between devices are 32-bit elements; how exact they have to be, the bound alone decides.
A program may use at most 256 MiB of HBM per device.

```python
import math
import jax
import jax.numpy as jnp
from jax import lax

NX = 128
NY = 64
FINE = 4
COARSE = 1
ITERS = 2
NZ = 128
SLICES = 8


def draw_source(key, part):
    rough = jnp.clip(jax.random.normal(key, (NZ, NY, NX), jnp.float32), -4.0, 4.0)
    return 0.5 * rough


def shard_levels(own_key, shape, shards, smallest, largest):
    def one(position, parts):
        draws = jax.random.uniform(jax.random.fold_in(jax.random.fold_in(own_key, 6), position), (parts,), jnp.float32, smallest / len(shards), largest / len(shards))
        return jnp.repeat(jnp.exp(draws), shape[position] // parts).reshape((-1,) + (1,) * (len(shape) - position - 1))

    level = one(*shards[0])
    for cut in shards[1:]:
        level = level * one(*cut)
    return level


def scatter_about(key, shape, deviation, most, split=(), kind=jnp.bfloat16):
    result = deviation * jax.random.normal(key, shape, jnp.float32)
    if split:
        result = result * shard_levels(key, shape, split, -0.22, 0.18)
    return jnp.clip(result, -most, most).astype(kind)


def setup_inputs(seed: int = 0) -> dict:
    key_of = jax.random.split(jax.random.key(seed), 4)
    return {
        "initial": scatter_about(key_of[0], (NZ, NY, NX), 1.0, 6.0, ((0, 32),), jnp.float32),
        "conductivity": jnp.clip(jnp.exp(math.log(4.0) - 2.7725887 * jax.random.uniform(key_of[1], (NZ, NY, NX), jnp.float32) ** shard_levels(key_of[1], (NZ, NY, NX), ((0, 32),), -0.2, 0.2)), 0.25, 4.0),
        "source": draw_source(jax.random.fold_in(key_of[3], 71), 0),
    }


vertical_ratio = 64.0
fine_dt = 0.5


def thomas(sub_diag, main_diag, super_diag, rhs_rows):
    zero_plane = jnp.zeros_like(rhs_rows[0])

    def forward_step(carried, entries):
        sweep_prev, value_prev = carried
        sub_row, main_row, super_row, rhs_row = entries
        pivot_value = main_row - sub_row * sweep_prev
        sweep_now = super_row / pivot_value
        value_now = (rhs_row - sub_row * value_prev) / pivot_value
        return (sweep_now, value_now), (sweep_now, value_now)

    ignored, (sweeps, values) = lax.scan(forward_step, (zero_plane, zero_plane), (sub_diag, main_diag, super_diag, rhs_rows))

    def backward_step(following, entries):
        sweep_now, value_now = entries
        current = value_now - sweep_now * following
        return current, current

    ignored, solved = lax.scan(backward_step, zero_plane, (sweeps, values), reverse=True)
    return solved


def harmonic(first_side, second_side):
    return 2.0 * first_side * second_side / (first_side + second_side)


def implicit(values, conductivity, axis_pos, factor):
    moved = jnp.moveaxis(values, axis_pos, 0)
    kappa_rows = jnp.moveaxis(conductivity, axis_pos, 0)
    padded = jnp.pad(kappa_rows, [(1, 1)] + [(0, 0)] * (kappa_rows.ndim - 1))
    sub_diag = -factor * harmonic(padded[:-2], padded[1:-1])
    super_diag = -factor * harmonic(padded[1:-1], padded[2:])
    main_diag = 1.0 - sub_diag - super_diag
    return jnp.moveaxis(thomas(sub_diag, main_diag, super_diag, moved), 0, axis_pos)


def reference(initial, conductivity, source):
    coarse_dt = FINE * fine_dt / COARSE

    def coarse(values):
        for step_count in range(COARSE):
            values = implicit(values + coarse_dt * source, conductivity, 2, coarse_dt)
            values = implicit(values, conductivity, 1, coarse_dt)
        return values

    def fine(values):
        for step_count in range(FINE):
            values = implicit(values + fine_dt * source, conductivity, 2, fine_dt)
            values = implicit(values, conductivity, 1, fine_dt)
            values = implicit(values, conductivity, 0, fine_dt * vertical_ratio)
        return values

    states = [initial]
    for section in range(SLICES):
        states.append(coarse(states[-1]))
    for parareal_turn in range(ITERS):
        refined = [fine(states[section]) for section in range(SLICES)]
        previous = [coarse(states[section]) for section in range(SLICES)]
        updated = [initial]
        for section in range(SLICES):
            updated.append(coarse(updated[-1]) + refined[section] - previous[section])
        states = updated
    return jnp.stack(states[1:])
```

```python
import jax
import jax.numpy as jnp
from jax import lax
from jax.experimental import pallas as pl
from jax.experimental.pallas import tpu as pltpu
from jax.sharding import PartitionSpec as P

MESH = pl.DeviceIdType.MESH
FINE = 4
ITERS = 2
SLICES = 8
NA = 8
NB = 4
BZ = 16
BY = 16
SLAB = 4
NX = 128
NY = 64
STEPS = ITERS * FINE
fine_dt = 0.5
coarse_dt = 2.0
vertical_ratio = 64.0


def harmonic(one, other):
    return 2.0 * one * other / (one + other)


def shift(values, amount, axis):
    return pltpu.roll(values, amount % values.shape[axis], axis)


def masked_faces(kappa, factor, axis):
    size = kappa.shape[axis]
    where = lax.broadcasted_iota(jnp.int32, kappa.shape, axis)
    faces = factor * harmonic(kappa, shift(kappa, -1, axis))
    return jnp.where(where == size - 1, 0.0, faces)


def cyclic_setup(faces, axis, store):
    size = faces.shape[axis]
    below = shift(faces, 1, axis)
    main = 1.0 + faces + below
    low, high = -below, -faces
    level, stride = 0, 1
    while stride < size:
        inverse = 1.0 / main
        alpha = -low * shift(inverse, stride, axis)
        beta = -high * shift(inverse, -stride, axis)
        store(level, alpha, beta)
        main = main + alpha * low + beta * high
        low, high = (alpha * shift(low, stride, axis), beta * shift(high, -stride, axis))
        level, stride = level + 1, stride * 2
    store(None, 1.0 / main, None)


def cyclic_apply(values, axis, alpha, beta, inverse):
    size = values.shape[axis]
    level, stride = 0, 1
    while stride < size:
        values = (
            values
            + alpha(level) * shift(values, stride, axis)
            + beta(level) * shift(values, -stride, axis)
        )
        level, stride = level + 1, stride * 2
    return values * inverse


def tree_sum(terms):
    terms = list(terms)
    while len(terms) > 1:
        terms = [
            terms[i] + terms[i + 1] if i + 1 < len(terms) else terms[i]
            for i in range(0, len(terms), 2)
        ]
    return terms[0]


def kernel(
    init_ref, kap_ref, src_ref, out_ref,
    Kb, Sb, Kz, Gz, Gy, tz_s, tz_r, ty_s, ty_r,
    Ew, Lw, Uw, Mw, Cz, Cy, Wz, Wy, Xc, CXc, CYc,
    V, Fs, ST, FB, UB, mz_s, mz_r, my_s, my_r,
    r0, s0, r1, s1, rz, szm, ry, sym, rF, sF, rS, sS, rO, sO,
):
    t = lax.axis_index("tm")
    p = lax.axis_index("pencil")
    a = lax.div(p, 4)
    b = lax.rem(p, 4)
    layer_own = lax.div(t, 2)
    is_owner = lax.rem(t, 2) == 0

    def at_z(da, bb):
        return (t, 4 * lax.rem(a + da, NA) + bb)

    def send(src, dst, ssem, rsem, dev):
        pltpu.make_async_remote_copy(
            src_ref=src, dst_ref=dst, send_sem=ssem, recv_sem=rsem,
            device_id=dev, device_id_type=MESH,
        ).start()

    def wait_bytes(ref, sem):
        pltpu.make_async_copy(ref, ref, sem).wait()

    barrier = pltpu.get_barrier_semaphore()

    def greet_plane(i, c):
        g = lax.rem(t * NB + b + i, SLICES * NB)
        pl.semaphore_signal(
            barrier, inc=1, device_id=(lax.div(g, NB), 4 * a + lax.rem(g, NB)), device_id_type=MESH
        )
        return c

    def greet_ring(i, c):
        pl.semaphore_signal(barrier, inc=1, device_id=at_z(i, b), device_id_type=MESH)
        return c

    def greet_side(i, c):
        other = lax.rem(b + i, NB)
        pl.semaphore_signal(barrier, inc=1, device_id=at_z(1, other), device_id_type=MESH)
        pl.semaphore_signal(barrier, inc=1, device_id=at_z(NA - 1, other), device_id_type=MESH)
        return c

    lax.fori_loop(1, SLICES * NB, greet_plane, 0)
    lax.fori_loop(1, NA, greet_ring, 0)
    lax.fori_loop(1, NB, greet_side, 0)
    pl.semaphore_wait(barrier, (SLICES * NB - 1) + (NA - 1) + 2 * (NB - 1))

    def window(bb):
        return pl.multiple_of(jnp.minimum(jnp.maximum(16 * bb - 8, 0), 32), 8)

    mine = pl.ds(4 * b, SLAB)
    for i in range(1, NB):
        other = lax.rem(b + i, NB)
        send(kap_ref.at[:, pl.ds(window(other), 32), :], Kb.at[mine], s0.at[0], r0.at[0], at_z(0, other))
    for side, layer, da in ((3, SLAB - 1, 1), (0, 0, NA - 1)):

        @pl.when(b == side)
        def _():
            for other in range(NB):
                send(
                    kap_ref.at[layer, pl.ds(16 * other, 16), :],
                    Kz.at[0 if side == 3 else 1],
                    s0.at[2], r0.at[2 if side == 3 else 3], at_z(da, other),
                )

    for i in range(1, NB):
        other = lax.rem(b + i, NB)
        send(
            src_ref.at[:, pl.ds(pl.multiple_of(16 * other, 16), 16), :],
            Sb.at[mine], s0.at[1], r0.at[1], at_z(0, other),
        )
    pltpu.make_async_copy(kap_ref.at[:, pl.ds(window(b), 32), :], Kb.at[mine], r0.at[0]).start()
    pltpu.make_async_copy(
        src_ref.at[:, pl.ds(pl.multiple_of(16 * b, 16), 16), :], Sb.at[mine], r0.at[1]
    ).start()

    @pl.when(is_owner)
    def _():
        kappa = kap_ref[layer_own]

        def keep_x(level, one, other):
            if level is None:
                CXc[14] = one
            else:
                CXc[2 * level] = one
                CXc[2 * level + 1] = other

        def keep_y(level, one, other):
            if level is None:
                CYc[12] = one
            else:
                CYc[2 * level] = one
                CYc[2 * level + 1] = other

        cyclic_setup(masked_faces(kappa, coarse_dt, 1), 1, keep_x)
        cyclic_setup(masked_faces(kappa, coarse_dt, 0), 0, keep_y)

    def coarse(values):
        values = cyclic_apply(values, 1, lambda l: CXc[2 * l], lambda l: CXc[2 * l + 1], CXc[14])
        return cyclic_apply(values, 0, lambda l: CYc[2 * l], lambda l: CYc[2 * l + 1], CYc[12])

    wait_bytes(Kb, r0.at[0])
    wait_bytes(Kz.at[0], r0.at[2])
    wait_bytes(Kz.at[1], r0.at[3])
    row0 = 16 * b - window(b)

    def kappa_z(z):
        return Kb[pl.ds(pl.multiple_of(z * 32 + row0, 8), 16), :]

    def kappa_y(y):
        return Kb2[pl.ds(jnp.minimum(jnp.maximum(row0 + y, 0), 31), 16, stride=32), :]

    Kb2 = Kb.reshape(BZ * 32, NX)
    kappa_z = lambda z: Kb2[pl.ds(pl.multiple_of(z * 32 + row0, 8), 16), :]

    def two_port(G, ts, first, inner, last, lowest, highest, factor, length):
        previous = first
        for i in range(length + 1):
            following = inner(i) if i < length else last
            face = factor * harmonic(previous, following)
            if i == 0:
                face = jnp.where(lowest, 0.0, face)
            if i == length:
                face = jnp.where(highest, 0.0, face)
            G[i] = face
            previous = following
        link = G[0]
        ground_low = jnp.zeros_like(link)
        ground_high = jnp.ones_like(link)
        for i in range(1, length):
            face = G[i]
            part = 1.0 / (link + ground_high + face)
            ground_low = ground_low + link * ground_high * part
            ground_high_new = 1.0 + face * ground_high * part
            link = link * face * part
            ground_high = ground_high_new
        ts[0] = ground_low
        ts[1] = link
        ts[2] = ground_high

    two_port(Gz, tz_s, Kz[0], kappa_z, Kz[1], a == 0, a == NA - 1, fine_dt * vertical_ratio, BZ)
    for i in range(1, NA):
        send(tz_s, tz_r.at[a], s1.at[0], r1.at[0], at_z(i, b))
    two_port(Gy, ty_s, kappa_y(-1), kappa_y, kappa_y(BY), b == 0, b == NB - 1, fine_dt, BY)
    for i in range(1, NB):
        send(ty_s, ty_r.at[b], s1.at[1], r1.at[1], at_z(0, lax.rem(b + i, NB)))
    pltpu.make_async_copy(tz_s, tz_r.at[a], r1.at[0]).start()
    pltpu.make_async_copy(ty_s, ty_r.at[b], r1.at[1]).start()

    def give(it, n):
        for other in range(NB):
            src = UB.at[it, n, pl.ds(16 * other, 16), :]
            dst = ST.at[BZ * it + 4 * b + layer_own]
            own = jnp.logical_and(n == t, other == b)

            @pl.when(own)
            def _():
                pltpu.make_async_copy(src, dst, rS.at[it]).start()

            @pl.when(jnp.logical_not(own))
            def _():
                send(src, dst, sS.at[it], rS.at[it], (n, 4 * a + other))

    @pl.when(is_owner)
    def _():
        heat = coarse_dt * src_ref[layer_own]
        UB[0, 0] = init_ref[layer_own]
        UB[1, 0] = init_ref[layer_own]
        give(0, 0)

        def advance(n, c):
            UB[0, n] = coarse(UB[0, n - 1] + heat)
            give(0, n)
            return c

        lax.fori_loop(1, SLICES, advance, 0)
        UB[0, SLICES] = coarse(UB[0, SLICES - 1] + heat)

    for z in range(BZ):
        kappa = kappa_z(z)

        def keep(level, one, other, z=z):
            if level is None:
                Xc[14, 16 * z : 16 * z + 16] = one
            else:
                Xc[2 * level, 16 * z : 16 * z + 16] = one
                Xc[2 * level + 1, 16 * z : 16 * z + 16] = other

        cyclic_setup(masked_faces(kappa, fine_dt, 1), 1, keep)

    def split_setup(G, tr, C, W, place, count, length):
        down = jnp.ones_like(G[0])
        Ew[0] = down
        for j in range(count):
            ground_low, link, ground_high = tr[j, 0], tr[j, 1], tr[j, 2]
            passed = link / (link + ground_low + down)
            Mw[j] = passed
            down = ground_high + passed * (ground_low + down)
            Ew[j + 1] = down
        up = jnp.zeros_like(down)
        for j in range(count - 1, -1, -1):
            ground_low, link, ground_high = tr[j, 0], tr[j, 1], tr[j, 2]
            Uw[j] = up
            passed = link / (link + ground_high + up)
            Lw[j] = passed
            up = ground_low + passed * (ground_high + up)
        one = jnp.ones_like(down)
        below, above = [None], [None]
        w = jnp.where(place >= 1, one, 0.0)
        below.append(w)
        for i in range(2, count):
            w = w * Lw[lax.rem(place + count - i + 1, count)]
            below.append(jnp.where(place >= i, w, 0.0))
        w = one
        above.append(jnp.where(place + 1 < count, w, 0.0))
        for i in range(2, count):
            w = w * Mw[lax.rem(place + i - 1, count)]
            above.append(jnp.where(place + i < count, w, 0.0))
        for i in range(1, count):
            W[i - 1] = below[count - i]
            W[count - 1 + i - 1] = above[i]
        under = Ew[place]
        over = Uw[place]
        floor = G[0]
        seen = 1.0 + floor * under / (floor + under)
        last = length - 1
        for i in range(length - 1):
            face = G[i + 1]
            inverse = 1.0 / (face + seen)
            C[1, i] = inverse
            C[0, i] = face * inverse
            seen = 1.0 + face * seen * inverse
        C[1, last] = 1.0 / (seen + over)
        part = one
        C[3, last] = part
        for i in range(length - 2, -1, -1):
            part = part * C[0, i]
            C[3, i] = part
        seen = 1.0 + over
        steps = [None] * length
        for i in range(length - 2, -1, -1):
            face = G[i + 1]
            inverse = 1.0 / (face + seen)
            steps[i + 1] = face * inverse
            seen = 1.0 + face * seen * inverse
        part = floor / (floor + seen)
        C[2, 0] = part
        for i in range(1, length):
            part = part * steps[i]
            C[2, i] = part
        C[0, last] = (floor + seen) / (seen * (floor + under) + floor * under)

    wait_bytes(tz_r, r1.at[0])
    split_setup(Gz, tz_r, Cz, Wz, a, NA, BZ)
    wait_bytes(ty_r, r1.at[1])
    split_setup(Gy, ty_r, Cy, Wy, b, NB, BY)
    wait_bytes(Sb, r0.at[1])

    def split_apply(load, store, C, W, ms, mr, ssem, rsem, st, place, count, length, device):
        rows = [load(i) for i in range(length)]
        last = length - 1
        ms[st, 0] = C[1, last] * tree_sum(C[3, i] * rows[i] for i in range(length))
        ms[st, 1] = C[0, last] * tree_sum(C[2, i] * rows[i] for i in range(length))
        for i in range(1, count):
            which = jnp.where(place + i < count, 0, 1)
            send(ms.at[st, which], mr.at[st, count - 1 - i], ssem.at[st], rsem.at[st], device(i))
        swept = [rows[0]]
        for i in range(1, length):
            swept.append(rows[i] + C[0, i - 1] * swept[i - 1])
        solved = [None] * length
        solved[last] = C[1, last] * swept[last]
        for i in range(length - 2, -1, -1):
            solved[i] = C[1, i] * swept[i] + C[0, i] * solved[i + 1]
        wait_bytes(mr.at[st], rsem.at[st])
        got = [mr[st, i] for i in range(count - 1)]
        low = tree_sum(W[i] * got[i] for i in range(count - 1))
        high = tree_sum(W[count - 1 + i] * got[i] for i in range(count - 1))
        for i in range(length):
            store(i, solved[i] + C[2, i] * low + C[3, i] * high)

    def fine_step(it, s):
        st = it * FINE + s
        for z in range(0, BZ, 2):
            rows = pl.ds(16 * z, 32)
            start = V[rows] + fine_dt * Sb[z : z + 2].reshape(32, NX)
            V[rows] = cyclic_apply(
                start, 1, lambda l: Xc[2 * l, rows], lambda l: Xc[2 * l + 1, rows], Xc[14, rows]
            )

        def store_y(y, value):
            V[pl.ds(y, BZ, stride=BY), :] = value

        split_apply(
            lambda y: V[pl.ds(y, BZ, stride=BY), :], store_y,
            Cy, Wy, my_s, my_r, sym, ry, st, b, NB, BY, lambda i: at_z(0, lax.rem(b + i, NB)),
        )

        def store_z(z, value):
            V[pl.ds(16 * z, 16), :] = value

        split_apply(
            lambda z: V[pl.ds(16 * z, 16), :], store_z,
            Cz, Wz, mz_s, mz_r, szm, rz, st, a, NA, BZ, lambda i: at_z(i, b),
        )

    for it in range(ITERS):
        wait_bytes(ST.at[pl.ds(BZ * it, BZ)], rS.at[it])
        for z in range(BZ):
            V[pl.ds(16 * z, 16), :] = ST[BZ * it + z]

        def one_step(s, c):
            fine_step(it, s)
            return c

        lax.fori_loop(0, FINE, one_step, 0)
        for z in range(BZ):
            Fs[it, z] = V[pl.ds(16 * z, 16), :]

        def hand_in(l, c):
            other = lax.div(l, 4)
            target = 2 * lax.rem(l, 4)
            dst = FB.at[it, t, pl.ds(pl.multiple_of(16 * b, 16), 16), :]
            own = jnp.logical_and(target == t, other == b)

            @pl.when(own)
            def _():
                pltpu.make_async_copy(Fs.at[it, l], dst, rF.at[it, t]).start()

            @pl.when(jnp.logical_not(own))
            def _():
                send(Fs.at[it, l], dst, sF.at[it], rF.at[it, t], (target, 4 * a + other))

            return c

        lax.fori_loop(0, BZ, hand_in, 0)

        @pl.when(is_owner)
        def _():
            last_turn = it == ITERS - 1

            def finish(n, value):
                UB[it + 1, n + 1] = UB[it, n + 1] + value
                if last_turn:
                    src = UB.at[it + 1, n + 1]
                    dst = out_ref.at[0, layer_own]

                    @pl.when(n == t)
                    def _():
                        pltpu.make_async_copy(src, dst, rO).start()

                    @pl.when(n != t)
                    def _():
                        send(src, dst, sO, rO, (n, p))

            def correct(n, before):
                wait_bytes(FB.at[it, n], rF.at[it, n])
                value = coarse(before) + (FB[it, n] - UB[it, n + 1])
                finish(n, value)
                if not last_turn:
                    @pl.when(n + 1 < SLICES)
                    def _():
                        give(it + 1, n + 1)
                return value

            if not last_turn:
                give(it + 1, 0)
            lax.fori_loop(0, SLICES, correct, jnp.zeros((NY, NX), jnp.float32))

    wait_bytes(out_ref, rO)
    wait_bytes(Kb.at[pl.ds(0, 12)], s0.at[0])
    wait_bytes(Sb.at[pl.ds(0, 12)], s0.at[1])

    @pl.when(jnp.logical_or(b == 0, b == NB - 1))
    def _():
        wait_bytes(ST.at[pl.ds(0, NB)], s0.at[2])

    wait_bytes(tz_r.at[pl.ds(0, NA - 1)], s1.at[0])
    wait_bytes(ty_r.at[pl.ds(0, NB - 1)], s1.at[1])

    def drain(st, c):
        wait_bytes(mz_r.at[st], szm.at[st])
        wait_bytes(my_r.at[st], sym.at[st])
        return c

    lax.fori_loop(0, STEPS, drain, 0)
    for it in range(ITERS):

        @pl.when(is_owner)
        def _():
            wait_bytes(Fs.at[it, pl.ds(0, BZ - 1)], sF.at[it])
            wait_bytes(ST.at[pl.ds(0, 31)], sS.at[it])

        @pl.when(jnp.logical_not(is_owner))
        def _():
            wait_bytes(Fs.at[it], sF.at[it])

    @pl.when(is_owner)
    def _():
        wait_bytes(FB.at[0, pl.ds(0, SLICES - 1)], sO)


def vm(*shape):
    return pltpu.VMEM(shape, jnp.float32)


def per_device(initial, conductivity, source):
    dma = pltpu.SemaphoreType.DMA
    line = (16, NX)
    return pl.pallas_call(
        kernel,
        out_shape=jax.ShapeDtypeStruct((1, SLAB, NY, NX), jnp.float32),
        in_specs=[pl.BlockSpec(memory_space=pltpu.VMEM)] * 3,
        out_specs=pl.BlockSpec(memory_space=pltpu.VMEM),
        scratch_shapes=[
            vm(BZ, 32, NX), vm(BZ, BY, NX), vm(2, *line), vm(BZ + 1, *line), vm(BY + 1, *line),
            vm(3, *line), vm(NA, 3, *line), vm(3, *line), vm(NB, 3, *line),
            vm(NA + 1, *line), vm(NA, *line), vm(NA, *line), vm(NA, *line),
            vm(4, BZ, *line), vm(4, BY, *line), vm(2 * (NA - 1), *line), vm(2 * (NB - 1), *line),
            vm(15, BZ * BY, NX), vm(15, NY, NX), vm(13, NY, NX),
            vm(BZ * BY, NX), vm(ITERS, BZ, *line), vm(ITERS * BZ, *line),
            vm(ITERS, SLICES, NY, NX), vm(ITERS + 1, SLICES + 1, NY, NX),
            vm(STEPS, 2, *line), vm(STEPS, NA - 1, *line), vm(STEPS, 2, *line), vm(STEPS, NB - 1, *line),
            dma((4,)), dma((3,)), dma((2,)), dma((2,)),
            dma((STEPS,)), dma((STEPS,)), dma((STEPS,)), dma((STEPS,)),
            dma((ITERS, SLICES)), dma((ITERS,)), dma((ITERS,)), dma((ITERS,)), dma, dma,
        ],
        compiler_params=pltpu.CompilerParams(
            collective_id=0, has_side_effects=True, vmem_limit_bytes=40 * 1024 * 1024
        ),
        name="parareal",
    )(initial, conductivity, source)


def solution(mesh):
    placed = P("pencil", None, None)
    return jax.shard_map(
        per_device,
        mesh=mesh,
        in_specs=(placed, placed, placed),
        out_specs=P("tm", "pencil", None, None),
        check_vma=False,
    )
```

```python
import jax
import jax.numpy as jnp
from jax import lax
from jax.experimental import pallas as pl
from jax.experimental.pallas import tpu as pltpu
from jax.sharding import PartitionSpec as P

MESH = pl.DeviceIdType.MESH
FINE = 4
ITERS = 2
SLICES = 8
NA = 8
NB = 4
NC = 2
BZ = 16
BY = 32
SLAB = 4
NX = 128
NY = 64
WIN = BY + 8
STEPS = ITERS * FINE
FAR_FIRST = (4, 3, 5, 2, 6, 1, 7)
fine_dt = 0.5
coarse_dt = 2.0
vertical_ratio = 64.0


def harmonic(one, other):
    return 2.0 * one * other / (one + other)


def tree_sum(terms):
    terms = list(terms)
    while len(terms) > 1:
        terms = [
            terms[i] + terms[i + 1] if i + 1 < len(terms) else terms[i]
            for i in range(0, len(terms), 2)
        ]
    return terms[0]


def turn(values, amount):
    grouped = values.reshape(-1, 8, NX)
    return pltpu.roll(grouped, amount % 8, 1).reshape(values.shape)


def block_ends(faces, length):
    link = faces[0]
    ground_low = jnp.zeros_like(link)
    ground_high = jnp.ones_like(link)
    for i in range(1, length):
        face = faces[i]
        part = 1.0 / (link + ground_high + face)
        ground_low = ground_low + link * ground_high * part
        ground_high, link = (1.0 + face * ground_high * part, link * face * part)
    return ground_low, link, ground_high


def block_coefficients(faces, under, over, length, C):
    floor = faces[0]
    seen = 1.0 + floor * under / (floor + under)
    last = length - 1
    for i in range(last):
        face = faces[i + 1]
        inverse = 1.0 / (face + seen)
        C[1, i] = inverse
        C[0, i] = face * inverse
        seen = 1.0 + face * seen * inverse
    C[1, last] = 1.0 / (seen + over)
    part = jnp.ones_like(floor)
    C[3, last] = part
    for i in range(last - 1, -1, -1):
        part = part * C[0, i]
        C[3, i] = part
    seen = 1.0 + over
    steps = [None] * length
    for i in range(last - 1, -1, -1):
        face = faces[i + 1]
        inverse = 1.0 / (face + seen)
        steps[i + 1] = face * inverse
        seen = 1.0 + face * seen * inverse
    part = floor / (floor + seen)
    C[2, 0] = part
    for i in range(1, length):
        part = part * steps[i]
        C[2, i] = part
    C[0, last] = (floor + seen) / (seen * (floor + under) + floor * under)


def block_edges(rows, C):
    last = len(rows) - 1
    return (
        C[1, last] * tree_sum(C[3, i] * row for i, row in enumerate(rows)),
        C[0, last] * tree_sum(C[2, i] * row for i, row in enumerate(rows)),
    )


def block_inner(rows, C):
    last = len(rows) - 1
    swept = [rows[0]]
    for i in range(1, last + 1):
        swept.append(rows[i] + C[0, i - 1] * swept[i - 1])
    solved = [None] * (last + 1)
    solved[last] = C[1, last] * swept[last]
    for i in range(last - 1, -1, -1):
        solved[i] = C[1, i] * swept[i] + C[0, i] * solved[i + 1]
    return solved


def local_setup(kappas, factor, C, W):
    length = len(kappas)
    position = lax.broadcasted_iota(jnp.int32, kappas[0].shape, 0) % 8
    faces = [None] + [
        factor * harmonic(kappas[i], kappas[i + 1]) for i in range(length - 1)
    ]
    top = factor * harmonic(kappas[length - 1], turn(kappas[0], -1))
    faces[0] = turn(jnp.where(position == 7, 0.0, top), 1)
    ground_low, link, ground_high = block_ends(faces, length)
    down = jnp.ones_like(link)
    for _ in range(8):
        under = turn(down, 1)
        down_part = link / (link + ground_low + under)
        down = ground_high + down_part * (ground_low + under)
    under = turn(down, 1)
    up = jnp.zeros_like(link)
    for _ in range(8):
        over = jnp.where(position == 7, 0.0, turn(up, -1))
        up_part = link / (link + ground_high + over)
        up = ground_low + up_part * (ground_high + over)
    over = jnp.where(position == 7, 0.0, turn(up, -1))
    low_part = link / (link + ground_high + over)
    high_part = link / (link + ground_low + under)
    below = jnp.ones_like(link)
    above = jnp.ones_like(link)
    for k in range(1, 8):
        if k > 1:
            below = below * turn(low_part, k - 1)
            above = above * turn(high_part, 1 - k)
        W[k - 1] = jnp.where(position >= k, below, 0.0)
        W[7 + k - 1] = jnp.where(position + k < 8, above, 0.0)
    block_coefficients(faces, under, over, length, C)


def local_apply(rows, C, W):
    up, down = block_edges(rows, C)
    low = tree_sum(W[k - 1] * turn(up, k) for k in range(1, 8))
    high = tree_sum(W[7 + k - 1] * turn(down, -k) for k in range(1, 8))
    solved = block_inner(rows, C)
    return [
        value + C[2, i] * low + C[3, i] * high for i, value in enumerate(solved)
    ]


def kernel(
    init_ref, kap_ref, src_ref, out_ref,
    Kb, Sb, Kz, Gz, Gy, tz_s, tz_r, ty_s, ty_r,
    Ez, Lz, Uz, Mz, Ey, Ly, Uy, My, Cz, Cy, Wz, Wy, Cx, Wx, T,
    Ki, Hi, CXc, WXc, CYc, WYc, Tc, Lc,
    ST, FB, UB, mz_s, mz_r, my_s, my_r,
    r0, s0, r1, s1, rz, szm, ry, sym, rF, sF, rS, sS, rO, sO, rI,
):
    t = lax.axis_index("tm")
    p = lax.axis_index("pencil")
    a = lax.div(p, NB)
    b = lax.rem(p, NB)
    y = lax.div(t, NC)
    half = lax.rem(t, NC)
    is_fine = lax.rem(b + y, 2) == 0
    is_owner = lax.rem(b + y, 2) == 1
    section = 2 * b + lax.div(y, 2)
    layer_own = 2 * lax.div(y, 2) + half

    def at_z(da):
        return (t, NB * lax.rem(a + da, NA) + b)

    def fine_device(n, h):
        bb = lax.div(n, 2)
        yy = lax.rem(bb, 2) + 2 * lax.rem(n, 2)
        return (NC * yy + h, NB * a + bb)

    def owner_device(bb, k):
        yy = lax.rem(bb + 1, 2) + 2 * lax.div(k, 2)
        return (NC * yy + lax.rem(k, 2), NB * a + bb)

    def send(src, dst, ssem, rsem, dev):
        pltpu.make_async_remote_copy(
            src_ref=src, dst_ref=dst, send_sem=ssem, recv_sem=rsem,
            device_id=dev, device_id_type=MESH,
        ).start()

    def wait_bytes(ref, sem):
        pltpu.make_async_copy(ref, ref, sem).wait()

    barrier = pltpu.get_barrier_semaphore()

    def greet_plane(i, c):
        g = lax.rem(t * NB + b + i, SLICES * NB)
        pl.semaphore_signal(
            barrier, inc=1, device_id=(lax.div(g, NB), NB * a + lax.rem(g, NB)), device_id_type=MESH
        )
        return c

    def greet_side(i, c):
        other = lax.rem(b + i, NB)
        for da in (1, NA - 1):
            pl.semaphore_signal(
                barrier, inc=1, device_id=(t, NB * lax.rem(a + da, NA) + other), device_id_type=MESH
            )
        return c

    for i in FAR_FIRST:
        pl.semaphore_signal(barrier, inc=1, device_id=at_z(i), device_id_type=MESH)
    lax.fori_loop(1, NB, greet_side, 0)
    lax.fori_loop(1, SLICES * NB, greet_plane, 0)

    @pl.when(is_owner)
    def _():
        pltpu.make_async_copy(kap_ref.at[layer_own], Ki.at[0], rI.at[0]).start()
        pltpu.make_async_copy(src_ref.at[layer_own], Ki.at[1], rI.at[1]).start()
        pltpu.make_async_copy(init_ref.at[layer_own], Ki.at[2], rI.at[2]).start()

    pl.semaphore_wait(barrier, (SLICES * NB - 1) + (NA - 1) + 2 * (NB - 1))

    first = pl.multiple_of(half * BY, 8)
    window = pl.ds(pl.multiple_of(half * (NY - WIN), 8), WIN)
    mine = pl.ds(SLAB * b, SLAB)
    even = lax.rem(y, 2)
    for i in range(2):
        target = even + 2 * i

        @pl.when(target != b)
        def _():
            send(kap_ref.at[:, window, :], Kb.at[mine], s0.at[0], r0.at[0], (t, NB * a + target))

        @pl.when(target == b)
        def _():
            pltpu.make_async_copy(kap_ref.at[:, window, :], Kb.at[mine], r0.at[0]).start()

    for side, layer, da in ((NB - 1, SLAB - 1, 1), (0, 0, NA - 1)):

        @pl.when(b == side)
        def _():
            for i in range(2):
                send(
                    kap_ref.at[layer, pl.ds(first, BY), :],
                    Kz.at[0 if da == 1 else 1],
                    s0.at[2], r0.at[2 if da == 1 else 3],
                    (t, NB * lax.rem(a + da, NA) + even + 2 * i),
                )

    for i in range(2):
        target = even + 2 * i

        @pl.when(target != b)
        def _():
            send(src_ref.at[:, pl.ds(first, BY), :], Sb.at[mine], s0.at[1], r0.at[1], (t, NB * a + target))

        @pl.when(target == b)
        def _():
            pltpu.make_async_copy(src_ref.at[:, pl.ds(first, BY), :], Sb.at[mine], r0.at[1]).start()

    def give(it, n):
        for h in range(NC):
            send(
                UB.at[it, n, pl.ds(BY * h, BY), :],
                ST.at[it, pl.ds(pl.multiple_of(BY * (SLAB * b + layer_own), BY), BY), :],
                sS.at[it], rS.at[it], fine_device(n, h),
            )

    def coarse(values):
        Tc[:, 0:NY] = values.T
        rows = [Tc[pl.ds(i, 8, stride=16), :] for i in range(16)]
        for i, row in enumerate(local_apply(rows, CXc, WXc)):
            Tc[pl.ds(i, 8, stride=16), :] = row
        Lc[...] = Tc[:, 0:NY].T
        rows = [Lc[pl.ds(i, 8, stride=8), :] for i in range(8)]
        for i, row in enumerate(local_apply(rows, CYc, WYc)):
            Lc[pl.ds(i, 8, stride=8), :] = row
        return Lc[...]

    @pl.when(is_owner)
    def _():
        wait_bytes(Ki.at[0], rI.at[0])
        wait_bytes(Ki.at[1], rI.at[1])
        wait_bytes(Ki.at[2], rI.at[2])
        UB[0, 0] = Ki[2]
        UB[1, 0] = Ki[2]
        UB[2, 0] = Ki[2]
        give(0, 0)
        Tc[...] = jnp.ones_like(Tc)
        Tc[:, 0:NY] = Ki[0].T
        local_setup([Tc[pl.ds(i, 8, stride=16), :] for i in range(16)], coarse_dt, CXc, WXc)
        Lc[...] = Ki[0]
        local_setup([Lc[pl.ds(i, 8, stride=8), :] for i in range(8)], coarse_dt, CYc, WYc)
        heat = coarse_dt * Ki[1]
        Hi[...] = heat

        def advance(n, c):
            UB[0, n] = coarse(UB[0, n - 1] + Hi[...])
            give(0, n)
            return c

        lax.fori_loop(1, SLICES, advance, 0)
        UB[0, SLICES] = coarse(UB[0, SLICES - 1] + Hi[...])

    def split_setup(faces, tr, E, L, U, M, C, W, place, count, length):
        down = jnp.ones_like(faces[0])
        E[0] = down
        for j in range(count):
            ground_low, link, ground_high = tr[j, 0], tr[j, 1], tr[j, 2]
            passed = link / (link + ground_low + down)
            M[j] = passed
            down = ground_high + passed * (ground_low + down)
            E[j + 1] = down
        up = jnp.zeros_like(down)
        for j in range(count - 1, -1, -1):
            ground_low, link, ground_high = tr[j, 0], tr[j, 1], tr[j, 2]
            U[j] = up
            passed = link / (link + ground_high + up)
            L[j] = passed
            up = ground_low + passed * (ground_high + up)
        one = jnp.ones_like(down)
        below, above = [None], [None]
        part = one
        for i in range(1, count):
            if i > 1:
                part = part * L[lax.rem(place + count - i + 1, count)]
            below.append(jnp.where(place >= i, part, 0.0))
        part = one
        for i in range(1, count):
            if i > 1:
                part = part * M[lax.rem(place + i - 1, count)]
            above.append(jnp.where(place + i < count, part, 0.0))
        for i in range(1, count):
            W[i - 1] = below[count - i]
            W[count - 1 + i - 1] = above[i]
        block_coefficients(faces, E[place], U[place], length, C)

    def split_apply(load, store, C, W, ms, mr, ssem, rsem, st, place, count, length, order, device):
        rows = [load(i) for i in range(length)]
        up, down = block_edges(rows, C)
        ms[st, 0] = up
        ms[st, 1] = down
        for i in order:
            which = jnp.where(place + i < count, 0, 1)
            send(ms.at[st, which], mr.at[st, count - 1 - i], ssem.at[st], rsem.at[st], device(i))
        solved = block_inner(rows, C)
        wait_bytes(mr.at[st], rsem.at[st])
        got = [mr[st, i] for i in range(count - 1)]
        low = tree_sum(W[i] * got[i] for i in range(count - 1))
        high = tree_sum(W[count - 1 + i] * got[i] for i in range(count - 1))
        for i in range(length):
            store(i, solved[i] + C[2, i] * low + C[3, i] * high)

    @pl.when(is_fine)
    def _():
        wait_bytes(Kb, r0.at[0])
        wait_bytes(Kz.at[0], r0.at[2])
        wait_bytes(Kz.at[1], r0.at[3])
        row0 = 8 * half
        rows_of_k = Kb.reshape(BZ * WIN, NX)

        def kappa_z(z):
            return rows_of_k[pl.ds(pl.multiple_of(z * WIN + row0, 8), BY), :]

        def kappa_y(i):
            return rows_of_k[pl.ds(jnp.clip(row0 + i, 0, WIN - 1), BZ, stride=WIN), :]

        def outside(G, ts, first_k, inner, last_k, lowest, highest, factor, length):
            previous = first_k
            for i in range(length + 1):
                following = inner(i) if i < length else last_k
                face = factor * harmonic(previous, following)
                if i == 0:
                    face = jnp.where(lowest, 0.0, face)
                if i == length:
                    face = jnp.where(highest, 0.0, face)
                G[i] = face
                previous = following
            for i, part in enumerate(block_ends(G, length)):
                ts[i] = part

        outside(Gz, tz_s, Kz[0], kappa_z, Kz[1], a == 0, a == NA - 1, fine_dt * vertical_ratio, BZ)
        for i in FAR_FIRST:
            send(tz_s, tz_r.at[a], s1.at[0], r1.at[0], at_z(i))
        pltpu.make_async_copy(tz_s, tz_r.at[a], r1.at[0]).start()
        outside(Gy, ty_s, kappa_y(-1), kappa_y, kappa_y(BY), half == 0, half == 1, fine_dt, BY)
        partner = (t + 1 - 2 * half, p)
        send(ty_s, ty_r.at[half], s1.at[1], r1.at[1], partner)
        pltpu.make_async_copy(ty_s, ty_r.at[half], r1.at[1]).start()

        for z in range(BZ):
            T[pl.ds(BY * z, BY), :] = kappa_z(z)
        for tile in range(4):
            T[pl.ds(NX * tile, NX), :] = T[pl.ds(NX * tile, NX), :].T
        local_setup([T[pl.ds(i, 32, stride=16), :] for i in range(16)], fine_dt, Cx, Wx)

        wait_bytes(ty_r, r1.at[1])
        split_setup(Gy, ty_r, Ey, Ly, Uy, My, Cy, Wy, half, NC, BY)
        wait_bytes(tz_r, r1.at[0])
        split_setup(Gz, tz_r, Ez, Lz, Uz, Mz, Cz, Wz, a, NA, BZ)
        wait_bytes(Sb, r0.at[1])
        for z in range(BZ):
            Sb[z] = fine_dt * Sb[z]

        def fine_step(it, s):
            st = it * FINE + s
            V = ST.at[it]
            for tile in range(4):
                start = V[pl.ds(NX * tile, NX), :] + Sb[4 * tile : 4 * tile + 4].reshape(NX, NX)
                T[pl.ds(NX * tile, NX), :] = start.T
            rows = [T[pl.ds(i, 32, stride=16), :] for i in range(16)]
            for i, row in enumerate(local_apply(rows, Cx, Wx)):
                T[pl.ds(i, 32, stride=16), :] = row
            for tile in range(4):
                V[pl.ds(NX * tile, NX), :] = T[pl.ds(NX * tile, NX), :].T

            def store_y(i, value):
                V[pl.ds(i, BZ, stride=BY), :] = value

            split_apply(
                lambda i: V[pl.ds(i, BZ, stride=BY), :], store_y,
                Cy, Wy, my_s, my_r, sym, ry, st, half, NC, BY, (1,), lambda i: partner,
            )

            def store_z(i, value):
                V[pl.ds(BY * i, BY), :] = value

            split_apply(
                lambda i: V[pl.ds(BY * i, BY), :], store_z,
                Cz, Wz, mz_s, mz_r, szm, rz, st, a, NA, BZ, FAR_FIRST, at_z,
            )

        for it in range(ITERS):
            wait_bytes(ST.at[it], rS.at[it])

            def one_step(s, c):
                fine_step(it, s)
                return c

            lax.fori_loop(0, FINE, one_step, 0)

            def hand_in(i, c):
                bb = lax.rem(b + 2 + i, NB)
                for k in range(SLAB):
                    send(
                        ST.at[it, pl.ds(pl.multiple_of(BY * (SLAB * bb + k), BY), BY), :],
                        FB.at[it, section, pl.ds(first, BY), :],
                        sF.at[it], rF.at[it, section], owner_device(bb, k),
                    )
                return c

            lax.fori_loop(0, NB, hand_in, 0)

    @pl.when(is_owner)
    def _():
        for it in range(ITERS):
            last_turn = it == ITERS - 1

            def correct(n, before):
                wait_bytes(FB.at[it, n], rF.at[it, n])
                value = coarse(before) + (FB[it, n] - UB[it, n + 1])
                UB[it + 1, n + 1] = UB[it, n + 1] + value
                if last_turn:
                    src = UB.at[it + 1, n + 1]
                    dst = out_ref.at[0, layer_own]

                    @pl.when(n == t)
                    def _():
                        pltpu.make_async_copy(src, dst, rO).start()

                    @pl.when(n != t)
                    def _():
                        send(src, dst, sO, rO, (n, p))
                else:

                    @pl.when(n + 1 < SLICES)
                    def _():
                        give(it + 1, n + 1)
                return value

            if not last_turn:
                give(it + 1, 0)
            lax.fori_loop(0, SLICES, correct, jnp.zeros((NY, NX), jnp.float32))

    wait_bytes(out_ref, rO)

    @pl.when(is_fine)
    def _():
        wait_bytes(Kb.at[pl.ds(0, SLAB)], s0.at[0])
        wait_bytes(Sb.at[pl.ds(0, SLAB)], s0.at[1])
        wait_bytes(tz_r.at[pl.ds(0, NA - 1)], s1.at[0])
        wait_bytes(ty_s, s1.at[1])

        def drain(st, c):
            wait_bytes(mz_r.at[st], szm.at[st])
            wait_bytes(my_r.at[st], sym.at[st])
            return c

        lax.fori_loop(0, STEPS, drain, 0)
        for it in range(ITERS):
            wait_bytes(ST.at[it], sF.at[it])

    @pl.when(jnp.logical_or(b == 0, b == NB - 1))
    def _():
        wait_bytes(Kz, s0.at[2])

    @pl.when(is_owner)
    def _():
        wait_bytes(Kb.at[pl.ds(0, 2 * SLAB)], s0.at[0])
        wait_bytes(Sb.at[pl.ds(0, 2 * SLAB)], s0.at[1])
        for it in range(ITERS):
            wait_bytes(ST.at[it], sS.at[it])
        wait_bytes(FB.at[0, pl.ds(0, SLICES - 1)], sO)


def vm(*shape):
    return pltpu.VMEM(shape, jnp.float32)


def per_device(initial, conductivity, source):
    dma = pltpu.SemaphoreType.DMA
    zl = (BY, NX)
    yl = (BZ, NX)
    return pl.pallas_call(
        kernel,
        out_shape=jax.ShapeDtypeStruct((1, SLAB, NY, NX), jnp.float32),
        in_specs=[pl.BlockSpec(memory_space=pl.ANY)] * 3,
        out_specs=pl.BlockSpec(memory_space=pl.ANY),
        scratch_shapes=[
            vm(BZ, WIN, NX), vm(BZ, BY, NX), vm(2, *zl), vm(BZ + 1, *zl), vm(BY + 1, *yl),
            vm(3, *zl), vm(NA, 3, *zl), vm(3, *yl), vm(NC, 3, *yl),
            vm(NA + 1, *zl), vm(NA, *zl), vm(NA, *zl), vm(NA, *zl),
            vm(NC + 1, *yl), vm(NC, *yl), vm(NC, *yl), vm(NC, *yl),
            vm(4, BZ, *zl), vm(4, BY, *yl), vm(2 * (NA - 1), *zl), vm(2 * (NC - 1), *yl),
            vm(4, 16, 32, NX), vm(14, 32, NX), vm(BZ * BY, NX),
            vm(3, NY, NX), vm(NY, NX), vm(4, 16, 8, NX), vm(14, 8, NX),
            vm(4, 8, 8, NX), vm(14, 8, NX), vm(NX, NX), vm(NY, NX),
            vm(ITERS, BZ * BY, NX), vm(ITERS, SLICES, NY, NX), vm(ITERS + 1, SLICES + 1, NY, NX),
            vm(STEPS, 2, *zl), vm(STEPS, NA - 1, *zl), vm(STEPS, 2, *yl), vm(STEPS, NC - 1, *yl),
            dma((4,)), dma((3,)), dma((2,)), dma((2,)),
            dma((STEPS,)), dma((STEPS,)), dma((STEPS,)), dma((STEPS,)),
            dma((ITERS, SLICES)), dma((ITERS,)), dma((ITERS,)), dma((ITERS,)), dma, dma, dma((3,)),
        ],
        compiler_params=pltpu.CompilerParams(
            collective_id=0, has_side_effects=True, vmem_limit_bytes=48 * 1024 * 1024
        ),
        name="parareal",
    )(initial, conductivity, source)


def solution(mesh):
    placed = P("pencil", None, None)
    return jax.shard_map(
        per_device,
        mesh=mesh,
        in_specs=(placed, placed, placed),
        out_specs=P("tm", "pencil", None, None),
        check_vma=False,
    )
```

```python
import jax
import jax.numpy as jnp
from jax import lax
from jax.experimental import pallas as pl
from jax.experimental.pallas import tpu as pltpu
from jax.sharding import PartitionSpec as P

MESH = pl.DeviceIdType.MESH
FINE = 4
ITERS = 2
SLICES = 8
NA = 8
NB = 4
NC = 2
BZ = 16
BY = 32
SLAB = 4
NX = 128
NY = 64
WIN = BY + 8
STEPS = ITERS * FINE
FAR_FIRST = (4, 3, 5, 2, 6, 1, 7)
fine_dt = 0.5
coarse_dt = 2.0
vertical_ratio = 64.0


def harmonic(one, other):
    return 2.0 * one * other / (one + other)


def tree_sum(terms):
    terms = list(terms)
    while len(terms) > 1:
        terms = [
            terms[i] + terms[i + 1] if i + 1 < len(terms) else terms[i]
            for i in range(0, len(terms), 2)
        ]
    return terms[0]


def turn(values, amount):
    grouped = values.reshape(-1, 8, NX)
    return pltpu.roll(grouped, amount % 8, 1).reshape(values.shape)


def block_ends(faces, length):
    link = faces[0]
    ground_low = jnp.zeros_like(link)
    ground_high = jnp.ones_like(link)
    for i in range(1, length):
        face = faces[i]
        part = 1.0 / (link + ground_high + face)
        ground_low = ground_low + link * ground_high * part
        ground_high, link = (1.0 + face * ground_high * part, link * face * part)
    return ground_low, link, ground_high


def block_coefficients(faces, under, over, length, C):
    floor = faces[0]
    seen = 1.0 + floor * under / (floor + under)
    last = length - 1
    for i in range(last):
        face = faces[i + 1]
        inverse = 1.0 / (face + seen)
        C[1, i] = inverse
        C[0, i] = face * inverse
        seen = 1.0 + face * seen * inverse
    C[1, last] = 1.0 / (seen + over)
    part = jnp.ones_like(floor)
    C[3, last] = part
    for i in range(last - 1, -1, -1):
        part = part * C[0, i]
        C[3, i] = part
    seen = 1.0 + over
    steps = [None] * length
    for i in range(last - 1, -1, -1):
        face = faces[i + 1]
        inverse = 1.0 / (face + seen)
        steps[i + 1] = face * inverse
        seen = 1.0 + face * seen * inverse
    part = floor / (floor + seen)
    C[2, 0] = part
    for i in range(1, length):
        part = part * steps[i]
        C[2, i] = part
    C[0, last] = (floor + seen) / (seen * (floor + under) + floor * under)


def block_edges(rows, C):
    last = len(rows) - 1
    return (
        C[1, last] * tree_sum(C[3, i] * row for i, row in enumerate(rows)),
        C[0, last] * tree_sum(C[2, i] * row for i, row in enumerate(rows)),
    )


def block_inner(rows, C):
    last = len(rows) - 1
    swept = [rows[0]]
    for i in range(1, last + 1):
        swept.append(rows[i] + C[0, i - 1] * swept[i - 1])
    solved = [None] * (last + 1)
    solved[last] = C[1, last] * swept[last]
    for i in range(last - 1, -1, -1):
        solved[i] = C[1, i] * swept[i] + C[0, i] * solved[i + 1]
    return solved


def local_setup(kappas, factor, C, W):
    length = len(kappas)
    position = lax.broadcasted_iota(jnp.int32, kappas[0].shape, 0) % 8
    faces = [None] + [
        factor * harmonic(kappas[i], kappas[i + 1]) for i in range(length - 1)
    ]
    top = factor * harmonic(kappas[length - 1], turn(kappas[0], -1))
    faces[0] = turn(jnp.where(position == 7, 0.0, top), 1)
    ground_low, link, ground_high = block_ends(faces, length)
    down = jnp.ones_like(link)
    for _ in range(8):
        under = turn(down, 1)
        down_part = link / (link + ground_low + under)
        down = ground_high + down_part * (ground_low + under)
    under = turn(down, 1)
    up = jnp.zeros_like(link)
    for _ in range(8):
        over = jnp.where(position == 7, 0.0, turn(up, -1))
        up_part = link / (link + ground_high + over)
        up = ground_low + up_part * (ground_high + over)
    over = jnp.where(position == 7, 0.0, turn(up, -1))
    low_part = link / (link + ground_high + over)
    high_part = link / (link + ground_low + under)
    below = jnp.ones_like(link)
    above = jnp.ones_like(link)
    for k in range(1, 8):
        if k > 1:
            below = below * turn(low_part, k - 1)
            above = above * turn(high_part, 1 - k)
        W[k - 1] = jnp.where(position >= k, below, 0.0)
        W[7 + k - 1] = jnp.where(position + k < 8, above, 0.0)
    block_coefficients(faces, under, over, length, C)


def local_apply(rows, C, W):
    up, down = block_edges(rows, C)
    low = tree_sum(W[k - 1] * turn(up, k) for k in range(1, 8))
    high = tree_sum(W[7 + k - 1] * turn(down, -k) for k in range(1, 8))
    solved = block_inner(rows, C)
    return [
        value + C[2, i] * low + C[3, i] * high for i, value in enumerate(solved)
    ]


def kernel(
    init_ref, kap_ref, src_ref, out_ref,
    Kb, Sb, Kz, Gz, Gy, tz_s, tz_r, ty_s, ty_r,
    Ez, Lz, Uz, Mz, Ey, Ly, Uy, My, Cz, Cy, Wz, Wy, Cx, Wx, T,
    Ki, Hi, CXc, WXc, CYc, WYc, Tc, Lc,
    ST, FB, UB, mz_s, mz_r, my_s, my_r,
    r0, s0, r1, s1, rz, szm, ry, sym, rF, sF, rS, sS, rO, sO, rI,
):
    t = lax.axis_index("tm")
    p = lax.axis_index("pencil")
    a = lax.div(p, NB)
    b = lax.rem(p, NB)
    y = lax.div(t, NC)
    half = lax.rem(t, NC)
    is_fine = lax.rem(b + y, 2) == 0
    odd = lax.rem(b + y, 2) == 1
    is_owner = jnp.logical_and(odd, half == 0)
    is_helper = jnp.logical_and(odd, half == 1)
    section = 2 * b + lax.div(y, 2)
    pair = lax.div(y, 2)
    owned = pl.ds(2 * pair, 2)

    def at_z(da):
        return (t, NB * lax.rem(a + da, NA) + b)

    def fine_device(n, h):
        bb = lax.div(n, 2)
        yy = lax.rem(bb, 2) + 2 * lax.rem(n, 2)
        return (NC * yy + h, NB * a + bb)

    def owner_device(bb, k):
        return (NC * (lax.rem(bb + 1, 2) + 2 * k), NB * a + bb)

    def send(src, dst, ssem, rsem, dev):
        pltpu.make_async_remote_copy(
            src_ref=src, dst_ref=dst, send_sem=ssem, recv_sem=rsem,
            device_id=dev, device_id_type=MESH,
        ).start()

    def wait_bytes(ref, sem):
        pltpu.make_async_copy(ref, ref, sem).wait()

    barrier = pltpu.get_barrier_semaphore()

    def greet(dev):
        pl.semaphore_signal(barrier, inc=1, device_id=dev, device_id_type=MESH)

    on_side = jnp.logical_or(b == 0, b == NB - 1)

    @pl.when(is_fine)
    def _():
        for i in FAR_FIRST:
            greet(at_z(i))

        @pl.when(b != NB - 1)
        def _():
            greet((t, NB * lax.rem(a + NA - 1, NA) + NB - 1))

        @pl.when(b != 0)
        def _():
            greet((t, NB * lax.rem(a + 1, NA)))

        greet((t, NB * a + lax.rem(b + 2, NB)))

        @pl.when(half == 1)
        def _():
            greet((t, NB * a + lax.rem(b + 1, NB)))
            greet((t, NB * a + lax.rem(b + 3, NB)))

        for i in (2, 1, 3, 0):
            for k in range(2):
                greet(owner_device(lax.rem(b + i, NB), k))
        greet((t + 1 - 2 * half, p))
        pl.semaphore_wait(barrier, (NA - 1) + 1 + 8 + 1 + jnp.where(on_side, 1, 0))

    @pl.when(is_owner)
    def _():
        def greet_slices(i, c):
            for h in range(NC):
                greet(fine_device(lax.rem(2 * b + 4 + i, SLICES), h))
            return c

        lax.fori_loop(0, SLICES, greet_slices, 0)
        greet(owner_device(b, 1 - pair))
        pltpu.make_async_copy(kap_ref.at[owned], Ki.at[0], rI.at[0]).start()
        pltpu.make_async_copy(src_ref.at[owned], Ki.at[1], rI.at[1]).start()
        pltpu.make_async_copy(init_ref.at[owned], Ki.at[2], rI.at[2]).start()
        pl.semaphore_wait(barrier, 16 + 3 + jnp.where(on_side, 2, 0))

    @pl.when(is_helper)
    def _():
        for k in range(2):
            greet(owner_device(b, k))
        pl.semaphore_wait(barrier, 2 + jnp.where(on_side, 2, 0))

    first = pl.multiple_of(half * BY, 8)
    window = pl.ds(pl.multiple_of(half * (NY - WIN), 8), WIN)
    mine = pl.ds(SLAB * b, SLAB)
    even = lax.rem(y, 2)
    for i in range(2):
        target = even + 2 * i

        @pl.when(target != b)
        def _():
            send(kap_ref.at[:, window, :], Kb.at[mine], s0.at[0], r0.at[0], (t, NB * a + target))

        @pl.when(target == b)
        def _():
            pltpu.make_async_copy(kap_ref.at[:, window, :], Kb.at[mine], r0.at[0]).start()

    for side, layer, da in ((NB - 1, SLAB - 1, 1), (0, 0, NA - 1)):

        @pl.when(b == side)
        def _():
            for i in range(2):
                send(
                    kap_ref.at[layer, pl.ds(first, BY), :],
                    Kz.at[0 if da == 1 else 1],
                    s0.at[2], r0.at[2 if da == 1 else 3],
                    (t, NB * lax.rem(a + da, NA) + even + 2 * i),
                )

    for i in range(2):
        target = even + 2 * i

        @pl.when(target != b)
        def _():
            send(src_ref.at[:, pl.ds(first, BY), :], Sb.at[mine], s0.at[1], r0.at[1], (t, NB * a + target))

        @pl.when(target == b)
        def _():
            pltpu.make_async_copy(src_ref.at[:, pl.ds(first, BY), :], Sb.at[mine], r0.at[1]).start()

    def give(it, n):
        for h in range(NC):
            send(
                UB.at[it, n, :, pl.ds(BY * h, BY), :],
                ST.at[it, pl.ds(SLAB * b + 2 * pair, 2)],
                sS.at[it], rS.at[it], fine_device(n, h),
            )

    def coarse(values):
        Tc[...] = values.reshape(2 * NY, NX).T
        rows = [Tc[pl.ds(i, 8, stride=16), :] for i in range(16)]
        for i, row in enumerate(local_apply(rows, CXc, WXc)):
            Tc[pl.ds(i, 8, stride=16), :] = row
        Lc[...] = Tc[...].T
        rows = [Lc[pl.ds(i, 16, stride=8), :] for i in range(8)]
        for i, row in enumerate(local_apply(rows, CYc, WYc)):
            Lc[pl.ds(i, 16, stride=8), :] = row
        return Lc[...].reshape(2, NY, NX)

    @pl.when(is_owner)
    def _():
        wait_bytes(Ki.at[0], rI.at[0])
        wait_bytes(Ki.at[1], rI.at[1])
        wait_bytes(Ki.at[2], rI.at[2])
        UB[0, 0] = Ki[2]
        UB[1, 0] = Ki[2]
        UB[2, 0] = Ki[2]
        give(0, 0)
        Lc[...] = Ki[0].reshape(2 * NY, NX)
        Tc[...] = Lc[...].T
        local_setup([Tc[pl.ds(i, 8, stride=16), :] for i in range(16)], coarse_dt, CXc, WXc)
        local_setup([Lc[pl.ds(i, 16, stride=8), :] for i in range(8)], coarse_dt, CYc, WYc)
        Hi[...] = coarse_dt * Ki[1]

        def advance(n, c):
            UB[0, n] = coarse(UB[0, n - 1] + Hi[...])
            give(0, n)
            return c

        lax.fori_loop(1, SLICES, advance, 0)
        UB[0, SLICES] = coarse(UB[0, SLICES - 1] + Hi[...])

    def split_setup(faces, tr, E, L, U, M, C, W, place, count, length):
        down = jnp.ones_like(faces[0])
        E[0] = down
        for j in range(count):
            ground_low, link, ground_high = tr[j, 0], tr[j, 1], tr[j, 2]
            passed = link / (link + ground_low + down)
            M[j] = passed
            down = ground_high + passed * (ground_low + down)
            E[j + 1] = down
        up = jnp.zeros_like(down)
        for j in range(count - 1, -1, -1):
            ground_low, link, ground_high = tr[j, 0], tr[j, 1], tr[j, 2]
            U[j] = up
            passed = link / (link + ground_high + up)
            L[j] = passed
            up = ground_low + passed * (ground_high + up)
        one = jnp.ones_like(down)
        below, above = [None], [None]
        part = one
        for i in range(1, count):
            if i > 1:
                part = part * L[lax.rem(place + count - i + 1, count)]
            below.append(jnp.where(place >= i, part, 0.0))
        part = one
        for i in range(1, count):
            if i > 1:
                part = part * M[lax.rem(place + i - 1, count)]
            above.append(jnp.where(place + i < count, part, 0.0))
        for i in range(1, count):
            W[i - 1] = below[count - i]
            W[count - 1 + i - 1] = above[i]
        block_coefficients(faces, E[place], U[place], length, C)

    def join(got, W):
        count = len(got)
        return (
            tree_sum(W[i] * got[i] for i in range(count)),
            tree_sum(W[count + i] * got[i] for i in range(count)),
        )

    @pl.when(is_fine)
    def _():
        wait_bytes(Kb, r0.at[0])
        wait_bytes(Kz.at[0], r0.at[2])
        wait_bytes(Kz.at[1], r0.at[3])
        row0 = 8 * half
        rows_of_k = Kb.reshape(BZ * WIN, NX)

        def kappa_z(z):
            return rows_of_k[pl.ds(pl.multiple_of(z * WIN + row0, 8), BY), :]

        def kappa_y(i):
            return rows_of_k[pl.ds(jnp.clip(row0 + i, 0, WIN - 1), BZ, stride=WIN), :]

        def outside(G, ts, first_k, inner, last_k, lowest, highest, factor, length):
            previous = first_k
            for i in range(length + 1):
                following = inner(i) if i < length else last_k
                face = factor * harmonic(previous, following)
                if i == 0:
                    face = jnp.where(lowest, 0.0, face)
                if i == length:
                    face = jnp.where(highest, 0.0, face)
                G[i] = face
                previous = following
            for i, part in enumerate(block_ends(G, length)):
                ts[i] = part

        outside(Gz, tz_s, Kz[0], kappa_z, Kz[1], a == 0, a == NA - 1, fine_dt * vertical_ratio, BZ)
        for i in FAR_FIRST:
            send(tz_s, tz_r.at[a], s1.at[0], r1.at[0], at_z(i))
        pltpu.make_async_copy(tz_s, tz_r.at[a], r1.at[0]).start()
        outside(Gy, ty_s, kappa_y(-1), kappa_y, kappa_y(BY), half == 0, half == 1, fine_dt, BY)
        partner = (t + 1 - 2 * half, p)
        send(ty_s, ty_r.at[half], s1.at[1], r1.at[1], partner)
        pltpu.make_async_copy(ty_s, ty_r.at[half], r1.at[1]).start()

        for z in range(BZ):
            T[pl.ds(BY * z, BY), :] = kappa_z(z)
        for tile in range(4):
            T[pl.ds(NX * tile, NX), :] = T[pl.ds(NX * tile, NX), :].T
        for g in range(2):
            local_setup(
                [T[pl.ds(2 * NX * g + i, 16, stride=16), :] for i in range(16)],
                fine_dt, Cx.at[g], Wx.at[g],
            )
        wait_bytes(ty_r, r1.at[1])
        split_setup(Gy, ty_r, Ey, Ly, Uy, My, Cy, Wy, half, NC, BY)
        wait_bytes(Sb, r0.at[1])
        for z in range(BZ):
            Sb[z] = fine_dt * Sb[z]

        def solve_xy(it, st):
            V = ST.at[it].reshape(BZ * BY, NX)
            for g in range(2):
                for tile in range(2 * g, 2 * g + 2):
                    start = V[pl.ds(NX * tile, NX), :] + Sb[4 * tile : 4 * tile + 4].reshape(NX, NX)
                    T[pl.ds(NX * tile, NX), :] = start.T
                rows = [T[pl.ds(2 * NX * g + i, 16, stride=16), :] for i in range(16)]
                for i, row in enumerate(local_apply(rows, Cx.at[g], Wx.at[g])):
                    T[pl.ds(2 * NX * g + i, 16, stride=16), :] = row
                for tile in range(2 * g, 2 * g + 2):
                    V[pl.ds(NX * tile, NX), :] = T[pl.ds(NX * tile, NX), :].T
                C = Cy.at[:, :, pl.ds(8 * g, 8), :]
                rows = [V[pl.ds(8 * BY * g + i, 8, stride=BY), :] for i in range(BY)]
                up, down = block_edges(rows, C)
                my_s[st, g] = jnp.where(half == 0, up, down)
                send(my_s.at[st, g], my_r.at[st, g], sym.at[st, g], ry.at[st, g], partner)
            for g in range(2):
                C = Cy.at[:, :, pl.ds(8 * g, 8), :]
                rows = [V[pl.ds(8 * BY * g + i, 8, stride=BY), :] for i in range(BY)]
                solved = block_inner(rows, C)
                wait_bytes(my_r.at[st, g], ry.at[st, g])
                got = my_r[st, g]
                low, high = (Wy[0, 8 * g : 8 * g + 8] * got, Wy[1, 8 * g : 8 * g + 8] * got)
                for i in range(BY):
                    V[pl.ds(8 * BY * g + i, 8, stride=BY), :] = (
                        solved[i] + C[2, i] * low + C[3, i] * high
                    )

        def solve_z(it, st):
            V = ST.at[it].reshape(BZ * BY, NX)
            rows = [V[pl.ds(BY * i, BY), :] for i in range(BZ)]
            up, down = block_edges(rows, Cz)
            mz_s[st, 0] = up
            mz_s[st, 1] = down
            for i in FAR_FIRST:
                which = jnp.where(a + i < NA, 0, 1)
                send(mz_s.at[st, which], mz_r.at[st, NA - 1 - i], szm.at[st], rz.at[st], at_z(i))
            solved = block_inner(rows, Cz)
            wait_bytes(mz_r.at[st], rz.at[st])
            low, high = join([mz_r[st, i] for i in range(NA - 1)], Wz)
            for i in range(BZ):
                V[pl.ds(BY * i, BY), :] = solved[i] + Cz[2, i] * low + Cz[3, i] * high

        for it in range(ITERS):
            wait_bytes(ST.at[it], rS.at[it])
            solve_xy(it, it * FINE)
            if it == 0:
                wait_bytes(tz_r, r1.at[0])
                split_setup(Gz, tz_r, Ez, Lz, Uz, Mz, Cz, Wz, a, NA, BZ)

            def one_step(s, c):
                solve_z(it, it * FINE + s)
                solve_xy(it, it * FINE + s + 1)
                return c

            lax.fori_loop(0, FINE - 1, one_step, 0)
            solve_z(it, it * FINE + FINE - 1)

            for i in (2, 1, 3, 0):
                bb = lax.rem(b + i, NB)
                for k in range(2):
                    send(
                        ST.at[it, pl.ds(SLAB * bb + 2 * k, 2)],
                        FB.at[it, section, :, pl.ds(first, BY), :],
                        sF.at[it], rF.at[it, section], owner_device(bb, k),
                    )

    @pl.when(is_owner)
    def _():
        for it in range(ITERS):
            last_turn = it == ITERS - 1

            def correct(n, before):
                wait_bytes(FB.at[it, n], rF.at[it, n])
                value = coarse(before) + (FB[it, n] - UB[it, n + 1])
                UB[it + 1, n + 1] = UB[it, n + 1] + value
                if last_turn:
                    src = UB.at[it + 1, n + 1]
                    dst = out_ref.at[0, owned]

                    @pl.when(n == t)
                    def _():
                        pltpu.make_async_copy(src, dst, rO).start()

                    @pl.when(n != t)
                    def _():
                        send(src, dst, sO, rO, (n, p))
                else:

                    @pl.when(n + 1 < SLICES)
                    def _():
                        give(it + 1, n + 1)
                return value

            if not last_turn:
                give(it + 1, 0)
            lax.fori_loop(0, SLICES, correct, jnp.zeros((2, NY, NX), jnp.float32))

    @pl.when(is_fine)
    def _():
        wait_bytes(Kb.at[pl.ds(0, SLAB)], s0.at[0])
        wait_bytes(Sb.at[pl.ds(0, SLAB)], s0.at[1])
        wait_bytes(tz_r.at[pl.ds(0, NA - 1)], s1.at[0])
        wait_bytes(ty_s, s1.at[1])

        def drain(st, c):
            wait_bytes(mz_r.at[st], szm.at[st])
            for g in range(2):
                wait_bytes(my_r.at[st, g], sym.at[st, g])
            return c

        lax.fori_loop(0, STEPS, drain, 0)
        for it in range(ITERS):
            wait_bytes(ST.at[it], sF.at[it])

    @pl.when(jnp.logical_or(b == 0, b == NB - 1))
    def _():
        wait_bytes(Kz, s0.at[2])

    @pl.when(odd)
    def _():
        wait_bytes(Kb.at[pl.ds(0, 2 * SLAB)], s0.at[0])
        wait_bytes(Sb.at[pl.ds(0, 2 * SLAB)], s0.at[1])

    @pl.when(is_owner)
    def _():
        for it in range(ITERS):
            wait_bytes(FB.at[it], sS.at[it])
        wait_bytes(FB.at[0, pl.ds(0, SLICES - 1)], sO)

    wait_bytes(out_ref, rO)


def vm(*shape):
    return pltpu.VMEM(shape, jnp.float32)


def per_device(initial, conductivity, source):
    dma = pltpu.SemaphoreType.DMA
    zl = (BY, NX)
    yl = (BZ, NX)
    return pl.pallas_call(
        kernel,
        out_shape=jax.ShapeDtypeStruct((1, SLAB, NY, NX), jnp.float32),
        in_specs=[pl.BlockSpec(memory_space=pl.ANY)] * 3,
        out_specs=pl.BlockSpec(memory_space=pl.ANY),
        scratch_shapes=[
            vm(BZ, WIN, NX), vm(BZ, BY, NX), vm(2, *zl), vm(BZ + 1, *zl), vm(BY + 1, *yl),
            vm(3, *zl), vm(NA, 3, *zl), vm(3, *yl), vm(NC, 3, *yl),
            vm(NA + 1, *zl), vm(NA, *zl), vm(NA, *zl), vm(NA, *zl),
            vm(NC + 1, *yl), vm(NC, *yl), vm(NC, *yl), vm(NC, *yl),
            vm(4, BZ, *zl), vm(4, BY, *yl), vm(2 * (NA - 1), *zl), vm(2 * (NC - 1), *yl),
            vm(2, 4, 16, 16, NX), vm(2, 14, 16, NX), vm(BZ * BY, NX),
            vm(3, 2, NY, NX), vm(2, NY, NX), vm(4, 16, 8, NX), vm(14, 8, NX),
            vm(4, 8, 16, NX), vm(14, 16, NX), vm(NX, 2 * NY), vm(2 * NY, NX),
            vm(ITERS, BZ, BY, NX), vm(ITERS, SLICES, 2, NY, NX), vm(ITERS + 1, SLICES + 1, 2, NY, NX),
            vm(STEPS, 2, *zl), vm(STEPS, NA - 1, *zl), vm(STEPS, 2, 8, NX), vm(STEPS, 2, 8, NX),
            dma((4,)), dma((3,)), dma((2,)), dma((2,)),
            dma((STEPS,)), dma((STEPS,)), dma((STEPS, 2)), dma((STEPS, 2)),
            dma((ITERS, SLICES)), dma((ITERS,)), dma((ITERS,)), dma((ITERS,)), dma, dma, dma((3,)),
        ],
        compiler_params=pltpu.CompilerParams(
            collective_id=0, has_side_effects=True, vmem_limit_bytes=48 * 1024 * 1024
        ),
        name="parareal",
    )(initial, conductivity, source)


def solution(mesh):
    placed = P("pencil", None, None)
    return jax.shard_map(
        per_device,
        mesh=mesh,
        in_specs=(placed, placed, placed),
        out_specs=P("tm", "pencil", None, None),
        check_vma=False,
    )
```

```python
import jax
import jax.numpy as jnp
from jax import lax
from jax.experimental import pallas as pl
from jax.experimental.pallas import tpu as pltpu
from jax.sharding import PartitionSpec as P

MESH = pl.DeviceIdType.MESH
FINE = 4
ITERS = 2
SLICES = 8
NA = 8
NB = 4
NC = 2
BZ = 16
BY = 32
SLAB = 4
NX = 128
NY = 64
WIN = BY + 8
STEPS = ITERS * FINE
FAR_FIRST = (4, 3, 5, 2, 6, 1, 7)
fine_dt = 0.5
coarse_dt = 2.0
vertical_ratio = 64.0


def harmonic(one, other):
    return 2.0 * one * other / (one + other)


def tree_sum(terms):
    terms = list(terms)
    while len(terms) > 1:
        terms = [
            terms[i] + terms[i + 1] if i + 1 < len(terms) else terms[i]
            for i in range(0, len(terms), 2)
        ]
    return terms[0]


def turn(values, amount):
    grouped = values.reshape(-1, 8, NX)
    return pltpu.roll(grouped, amount % 8, 1).reshape(values.shape)


def block_ends(faces, length):
    link = faces[0]
    ground_low = jnp.zeros_like(link)
    ground_high = jnp.ones_like(link)
    for i in range(1, length):
        face = faces[i]
        part = 1.0 / (link + ground_high + face)
        ground_low = ground_low + link * ground_high * part
        ground_high, link = (1.0 + face * ground_high * part, link * face * part)
    return ground_low, link, ground_high


def block_coefficients(faces, under, over, length, C):
    floor = faces[0]
    seen = 1.0 + floor * under / (floor + under)
    last = length - 1
    for i in range(last):
        face = faces[i + 1]
        inverse = 1.0 / (face + seen)
        C[1, i] = inverse
        C[0, i] = face * inverse
        seen = 1.0 + face * seen * inverse
    C[1, last] = 1.0 / (seen + over)
    part = jnp.ones_like(floor)
    C[3, last] = part
    for i in range(last - 1, -1, -1):
        part = part * C[0, i]
        C[3, i] = part
    seen = 1.0 + over
    steps = [None] * length
    for i in range(last - 1, -1, -1):
        face = faces[i + 1]
        inverse = 1.0 / (face + seen)
        steps[i + 1] = face * inverse
        seen = 1.0 + face * seen * inverse
    part = floor / (floor + seen)
    C[2, 0] = part
    for i in range(1, length):
        part = part * steps[i]
        C[2, i] = part
    C[0, last] = (floor + seen) / (seen * (floor + under) + floor * under)


def block_edges(rows, C):
    last = len(rows) - 1
    return (
        C[1, last] * tree_sum(C[3, i] * row for i, row in enumerate(rows)),
        C[0, last] * tree_sum(C[2, i] * row for i, row in enumerate(rows)),
    )


def block_inner(rows, C):
    last = len(rows) - 1
    swept = [rows[0]]
    for i in range(1, last + 1):
        swept.append(rows[i] + C[0, i - 1] * swept[i - 1])
    solved = [None] * (last + 1)
    solved[last] = C[1, last] * swept[last]
    for i in range(last - 1, -1, -1):
        solved[i] = C[1, i] * swept[i] + C[0, i] * solved[i + 1]
    return solved


def local_setup(kappas, factor, C, W):
    length = len(kappas)
    position = lax.broadcasted_iota(jnp.int32, kappas[0].shape, 0) % 8
    faces = [None] + [
        factor * harmonic(kappas[i], kappas[i + 1]) for i in range(length - 1)
    ]
    top = factor * harmonic(kappas[length - 1], turn(kappas[0], -1))
    faces[0] = turn(jnp.where(position == 7, 0.0, top), 1)
    ground_low, link, ground_high = block_ends(faces, length)
    down = jnp.ones_like(link)
    for _ in range(8):
        under = turn(down, 1)
        down_part = link / (link + ground_low + under)
        down = ground_high + down_part * (ground_low + under)
    under = turn(down, 1)
    up = jnp.zeros_like(link)
    for _ in range(8):
        over = jnp.where(position == 7, 0.0, turn(up, -1))
        up_part = link / (link + ground_high + over)
        up = ground_low + up_part * (ground_high + over)
    over = jnp.where(position == 7, 0.0, turn(up, -1))
    low_part = link / (link + ground_high + over)
    high_part = link / (link + ground_low + under)
    below = jnp.ones_like(link)
    above = jnp.ones_like(link)
    for k in range(1, 8):
        if k > 1:
            below = below * turn(low_part, k - 1)
            above = above * turn(high_part, 1 - k)
        W[k - 1] = jnp.where(position >= k, below, 0.0)
        W[7 + k - 1] = jnp.where(position + k < 8, above, 0.0)
    block_coefficients(faces, under, over, length, C)


def local_apply(rows, C, W):
    up, down = block_edges(rows, C)
    low = tree_sum(W[k - 1] * turn(up, k) for k in range(1, 8))
    high = tree_sum(W[7 + k - 1] * turn(down, -k) for k in range(1, 8))
    solved = block_inner(rows, C)
    return [
        value + C[2, i] * low + C[3, i] * high for i, value in enumerate(solved)
    ]


def kernel(
    init_ref, kap_ref, src_ref, out_ref,
    Kb, Sb, Kz, Gz, Gy, tz_s, tz_r, ty_s, ty_r,
    Ez, Lz, Uz, Mz, Ey, Ly, Uy, My, Cz, Cy, Wz, Wy, Cx, Wx, T,
    Ki, Hi, CXc, WXc, CYc, WYc, Tc, Lc,
    ST, FB, UB, mz_s, mz_r, my_s, my_r,
    r0, s0, r1, s1, rz, szm, ry, sym, rF, sF, rS, sS, rO, sO, rI, kap, src,
):
    t = lax.axis_index("tm")
    p = lax.axis_index("pencil")
    a = lax.div(p, NB)
    b = lax.rem(p, NB)
    y = lax.div(t, NC)
    half = lax.rem(t, NC)
    is_fine = lax.rem(b + y, 2) == 0
    odd = lax.rem(b + y, 2) == 1
    is_owner = jnp.logical_and(odd, half == 0)
    is_helper = jnp.logical_and(odd, half == 1)
    section = 2 * b + lax.div(y, 2)
    pair = lax.div(y, 2)
    owned = pl.ds(2 * pair, 2)

    def at_z(da):
        return (t, NB * lax.rem(a + da, NA) + b)

    def fine_device(n, h):
        bb = lax.div(n, 2)
        yy = lax.rem(bb, 2) + 2 * lax.rem(n, 2)
        return (NC * yy + h, NB * a + bb)

    def owner_device(bb, k):
        return (NC * (lax.rem(bb + 1, 2) + 2 * k), NB * a + bb)

    def send(src, dst, ssem, rsem, dev):
        pltpu.make_async_remote_copy(
            src_ref=src, dst_ref=dst, send_sem=ssem, recv_sem=rsem,
            device_id=dev, device_id_type=MESH,
        ).start()

    def wait_bytes(ref, sem):
        pltpu.make_async_copy(ref, ref, sem).wait()

    barrier = pltpu.get_barrier_semaphore()

    pltpu.make_async_copy(kap_ref, kap, rI.at[3]).start()
    pltpu.make_async_copy(src_ref, src, rI.at[4]).start()

    def greet(dev):
        pl.semaphore_signal(barrier, inc=1, device_id=dev, device_id_type=MESH)

    on_side = jnp.logical_or(b == 0, b == NB - 1)

    @pl.when(is_fine)
    def _():
        for i in FAR_FIRST:
            greet(at_z(i))

        @pl.when(b != NB - 1)
        def _():
            greet((t, NB * lax.rem(a + NA - 1, NA) + NB - 1))

        @pl.when(b != 0)
        def _():
            greet((t, NB * lax.rem(a + 1, NA)))

        greet((t, NB * a + lax.rem(b + 2, NB)))

        @pl.when(half == 1)
        def _():
            greet((t, NB * a + lax.rem(b + 1, NB)))
            greet((t, NB * a + lax.rem(b + 3, NB)))

        for i in (2, 1, 3, 0):
            for k in range(2):
                greet(owner_device(lax.rem(b + i, NB), k))
        greet((t + 1 - 2 * half, p))
        pl.semaphore_wait(barrier, (NA - 1) + 1 + 8 + 1 + jnp.where(on_side, 1, 0))

    @pl.when(is_owner)
    def _():
        def greet_slices(i, c):
            for h in range(NC):
                greet(fine_device(lax.rem(2 * b + 4 + i, SLICES), h))
            return c

        lax.fori_loop(0, SLICES, greet_slices, 0)
        greet(owner_device(b, 1 - pair))
        pltpu.make_async_copy(kap_ref.at[owned], Ki.at[0], rI.at[0]).start()
        pltpu.make_async_copy(src_ref.at[owned], Ki.at[1], rI.at[1]).start()
        pltpu.make_async_copy(init_ref.at[owned], Ki.at[2], rI.at[2]).start()
        pl.semaphore_wait(barrier, 16 + 3 + jnp.where(on_side, 2, 0))

    @pl.when(is_helper)
    def _():
        for k in range(2):
            greet(owner_device(b, k))
        pl.semaphore_wait(barrier, 2 + jnp.where(on_side, 2, 0))

    wait_bytes(kap, rI.at[3])
    first = pl.multiple_of(half * BY, 8)
    window = pl.ds(pl.multiple_of(half * (NY - WIN), 8), WIN)
    mine = pl.ds(SLAB * b, SLAB)
    even = lax.rem(y, 2)
    for i in range(2):
        target = even + 2 * i

        @pl.when(target != b)
        def _():
            send(kap.at[:, window, :], Kb.at[mine], s0.at[0], r0.at[0], (t, NB * a + target))

        @pl.when(target == b)
        def _():
            pltpu.make_async_copy(kap.at[:, window, :], Kb.at[mine], r0.at[0]).start()

    for side, layer, da in ((NB - 1, SLAB - 1, 1), (0, 0, NA - 1)):

        @pl.when(b == side)
        def _():
            for i in range(2):
                send(
                    kap.at[layer, pl.ds(first, BY), :],
                    Kz.at[0 if da == 1 else 1],
                    s0.at[2], r0.at[2 if da == 1 else 3],
                    (t, NB * lax.rem(a + da, NA) + even + 2 * i),
                )

    wait_bytes(src, rI.at[4])
    for i in range(2):
        target = even + 2 * i

        @pl.when(target != b)
        def _():
            send(src.at[:, pl.ds(first, BY), :], Sb.at[mine], s0.at[1], r0.at[1], (t, NB * a + target))

        @pl.when(target == b)
        def _():
            pltpu.make_async_copy(src.at[:, pl.ds(first, BY), :], Sb.at[mine], r0.at[1]).start()

    def give(it, n):
        for h in range(NC):
            send(
                UB.at[it, n, :, pl.ds(BY * h, BY), :],
                ST.at[it, pl.ds(SLAB * b + 2 * pair, 2)],
                sS.at[it], rS.at[it], fine_device(n, h),
            )

    def coarse(values):
        Tc[...] = values.reshape(2 * NY, NX).T
        rows = [Tc[pl.ds(i, 8, stride=16), :] for i in range(16)]
        for i, row in enumerate(local_apply(rows, CXc, WXc)):
            Tc[pl.ds(i, 8, stride=16), :] = row
        Lc[...] = Tc[...].T
        rows = [Lc[pl.ds(i, 16, stride=8), :] for i in range(8)]
        for i, row in enumerate(local_apply(rows, CYc, WYc)):
            Lc[pl.ds(i, 16, stride=8), :] = row
        return Lc[...].reshape(2, NY, NX)

    @pl.when(is_owner)
    def _():
        wait_bytes(Ki.at[0], rI.at[0])
        wait_bytes(Ki.at[1], rI.at[1])
        wait_bytes(Ki.at[2], rI.at[2])
        UB[0, 0] = Ki[2]
        UB[1, 0] = Ki[2]
        UB[2, 0] = Ki[2]
        give(0, 0)
        Lc[...] = Ki[0].reshape(2 * NY, NX)
        Tc[...] = Lc[...].T
        local_setup([Tc[pl.ds(i, 8, stride=16), :] for i in range(16)], coarse_dt, CXc, WXc)
        local_setup([Lc[pl.ds(i, 16, stride=8), :] for i in range(8)], coarse_dt, CYc, WYc)
        Hi[...] = coarse_dt * Ki[1]

        def advance(n, c):
            UB[0, n] = coarse(UB[0, n - 1] + Hi[...])
            give(0, n)
            return c

        lax.fori_loop(1, SLICES, advance, 0)
        UB[0, SLICES] = coarse(UB[0, SLICES - 1] + Hi[...])

    def split_setup(faces, tr, E, L, U, M, C, W, place, count, length):
        down = jnp.ones_like(faces[0])
        E[0] = down
        for j in range(count):
            ground_low, link, ground_high = tr[j, 0], tr[j, 1], tr[j, 2]
            passed = link / (link + ground_low + down)
            M[j] = passed
            down = ground_high + passed * (ground_low + down)
            E[j + 1] = down
        up = jnp.zeros_like(down)
        for j in range(count - 1, -1, -1):
            ground_low, link, ground_high = tr[j, 0], tr[j, 1], tr[j, 2]
            U[j] = up
            passed = link / (link + ground_high + up)
            L[j] = passed
            up = ground_low + passed * (ground_high + up)
        one = jnp.ones_like(down)
        below, above = [None], [None]
        part = one
        for i in range(1, count):
            if i > 1:
                part = part * L[lax.rem(place + count - i + 1, count)]
            below.append(jnp.where(place >= i, part, 0.0))
        part = one
        for i in range(1, count):
            if i > 1:
                part = part * M[lax.rem(place + i - 1, count)]
            above.append(jnp.where(place + i < count, part, 0.0))
        for i in range(1, count):
            W[i - 1] = below[count - i]
            W[count - 1 + i - 1] = above[i]
        block_coefficients(faces, E[place], U[place], length, C)

    def join(got, W):
        count = len(got)
        return (
            tree_sum(W[i] * got[i] for i in range(count)),
            tree_sum(W[count + i] * got[i] for i in range(count)),
        )

    @pl.when(is_fine)
    def _():
        wait_bytes(Kb, r0.at[0])
        wait_bytes(Kz.at[0], r0.at[2])
        wait_bytes(Kz.at[1], r0.at[3])
        row0 = 8 * half
        rows_of_k = Kb.reshape(BZ * WIN, NX)

        def kappa_z(z):
            return rows_of_k[pl.ds(pl.multiple_of(z * WIN + row0, 8), BY), :]

        def kappa_y(i):
            return rows_of_k[pl.ds(jnp.clip(row0 + i, 0, WIN - 1), BZ, stride=WIN), :]

        def outside(G, ts, first_k, inner, last_k, lowest, highest, factor, length):
            previous = first_k
            for i in range(length + 1):
                following = inner(i) if i < length else last_k
                face = factor * harmonic(previous, following)
                if i == 0:
                    face = jnp.where(lowest, 0.0, face)
                if i == length:
                    face = jnp.where(highest, 0.0, face)
                G[i] = face
                previous = following
            for i, part in enumerate(block_ends(G, length)):
                ts[i] = part

        outside(Gz, tz_s, Kz[0], kappa_z, Kz[1], a == 0, a == NA - 1, fine_dt * vertical_ratio, BZ)
        for i in FAR_FIRST:
            send(tz_s, tz_r.at[a], s1.at[0], r1.at[0], at_z(i))
        pltpu.make_async_copy(tz_s, tz_r.at[a], r1.at[0]).start()
        outside(Gy, ty_s, kappa_y(-1), kappa_y, kappa_y(BY), half == 0, half == 1, fine_dt, BY)
        partner = (t + 1 - 2 * half, p)
        send(ty_s, ty_r.at[half], s1.at[1], r1.at[1], partner)
        pltpu.make_async_copy(ty_s, ty_r.at[half], r1.at[1]).start()

        for z in range(BZ):
            T[pl.ds(BY * z, BY), :] = kappa_z(z)
        for tile in range(4):
            T[pl.ds(NX * tile, NX), :] = T[pl.ds(NX * tile, NX), :].T
        for g in range(2):
            local_setup(
                [T[pl.ds(2 * NX * g + i, 16, stride=16), :] for i in range(16)],
                fine_dt, Cx.at[g], Wx.at[g],
            )
        wait_bytes(ty_r, r1.at[1])
        split_setup(Gy, ty_r, Ey, Ly, Uy, My, Cy, Wy, half, NC, BY)
        wait_bytes(Sb, r0.at[1])
        for z in range(BZ):
            Sb[z] = fine_dt * Sb[z]

        def solve_xy(it, st):
            V = ST.at[it].reshape(BZ * BY, NX)
            for g in range(2):
                for tile in range(2 * g, 2 * g + 2):
                    start = V[pl.ds(NX * tile, NX), :] + Sb[4 * tile : 4 * tile + 4].reshape(NX, NX)
                    T[pl.ds(NX * tile, NX), :] = start.T
                rows = [T[pl.ds(2 * NX * g + i, 16, stride=16), :] for i in range(16)]
                for i, row in enumerate(local_apply(rows, Cx.at[g], Wx.at[g])):
                    T[pl.ds(2 * NX * g + i, 16, stride=16), :] = row
                for tile in range(2 * g, 2 * g + 2):
                    V[pl.ds(NX * tile, NX), :] = T[pl.ds(NX * tile, NX), :].T
                C = Cy.at[:, :, pl.ds(8 * g, 8), :]
                rows = [V[pl.ds(8 * BY * g + i, 8, stride=BY), :] for i in range(BY)]
                up, down = block_edges(rows, C)
                my_s[st, g] = jnp.where(half == 0, up, down)
                send(my_s.at[st, g], my_r.at[st, g], sym.at[st, g], ry.at[st, g], partner)
            for g in range(2):
                C = Cy.at[:, :, pl.ds(8 * g, 8), :]
                rows = [V[pl.ds(8 * BY * g + i, 8, stride=BY), :] for i in range(BY)]
                solved = block_inner(rows, C)
                wait_bytes(my_r.at[st, g], ry.at[st, g])
                got = my_r[st, g]
                low, high = (Wy[0, 8 * g : 8 * g + 8] * got, Wy[1, 8 * g : 8 * g + 8] * got)
                for i in range(BY):
                    V[pl.ds(8 * BY * g + i, 8, stride=BY), :] = (
                        solved[i] + C[2, i] * low + C[3, i] * high
                    )

        ring = [(i, at_z(i), jnp.where(a + i < NA, 0, 1)) for i in FAR_FIRST]

        def solve_z(it, st):
            V = ST.at[it].reshape(BZ * BY, NX)
            rows = [V[pl.ds(BY * i, BY), :] for i in range(BZ)]
            up, down = block_edges(rows, Cz)
            mz_s[st, 0] = up
            mz_s[st, 1] = down
            for i, device, which in ring:
                send(mz_s.at[st, which], mz_r.at[st, NA - 1 - i], szm.at[st], rz.at[st], device)
            solved = block_inner(rows, Cz)
            wait_bytes(mz_r.at[st], rz.at[st])
            low, high = join([mz_r[st, i] for i in range(NA - 1)], Wz)
            for i in range(BZ):
                V[pl.ds(BY * i, BY), :] = solved[i] + Cz[2, i] * low + Cz[3, i] * high

        for it in range(ITERS):
            wait_bytes(ST.at[it], rS.at[it])
            solve_xy(it, it * FINE)
            if it == 0:
                wait_bytes(tz_r, r1.at[0])
                split_setup(Gz, tz_r, Ez, Lz, Uz, Mz, Cz, Wz, a, NA, BZ)

            def one_step(s, c):
                solve_z(it, it * FINE + s)
                solve_xy(it, it * FINE + s + 1)
                return c

            lax.fori_loop(0, FINE - 1, one_step, 0)
            solve_z(it, it * FINE + FINE - 1)

            for i in (2, 1, 3, 0):
                bb = lax.rem(b + i, NB)
                for k in range(2):
                    send(
                        ST.at[it, pl.ds(SLAB * bb + 2 * k, 2)],
                        FB.at[it, section, :, pl.ds(first, BY), :],
                        sF.at[it], rF.at[it, section], owner_device(bb, k),
                    )

    @pl.when(is_owner)
    def _():
        for it in range(ITERS):
            last_turn = it == ITERS - 1

            def correct(n, before):
                wait_bytes(FB.at[it, n], rF.at[it, n])
                value = coarse(before) + (FB[it, n] - UB[it, n + 1])
                UB[it + 1, n + 1] = UB[it, n + 1] + value
                if last_turn:
                    done = UB.at[it + 1, n + 1]
                    dst = out_ref.at[0, owned]

                    @pl.when(n == t)
                    def _():
                        pltpu.make_async_copy(done, dst, rO).start()

                    @pl.when(n != t)
                    def _():
                        send(done, dst, sO, rO, (n, p))
                else:

                    @pl.when(n + 1 < SLICES)
                    def _():
                        give(it + 1, n + 1)
                return value

            if not last_turn:
                give(it + 1, 0)
            lax.fori_loop(0, SLICES, correct, jnp.zeros((2, NY, NX), jnp.float32))

    @pl.when(is_fine)
    def _():
        wait_bytes(Kb.at[pl.ds(0, SLAB)], s0.at[0])
        wait_bytes(Sb.at[pl.ds(0, SLAB)], s0.at[1])
        wait_bytes(tz_r.at[pl.ds(0, NA - 1)], s1.at[0])
        wait_bytes(ty_s, s1.at[1])

        def drain(st, c):
            wait_bytes(mz_r.at[st], szm.at[st])
            for g in range(2):
                wait_bytes(my_r.at[st, g], sym.at[st, g])
            return c

        lax.fori_loop(0, STEPS, drain, 0)
        for it in range(ITERS):
            wait_bytes(ST.at[it], sF.at[it])

    @pl.when(jnp.logical_or(b == 0, b == NB - 1))
    def _():
        wait_bytes(Kz, s0.at[2])

    @pl.when(odd)
    def _():
        wait_bytes(Kb.at[pl.ds(0, 2 * SLAB)], s0.at[0])
        wait_bytes(Sb.at[pl.ds(0, 2 * SLAB)], s0.at[1])

    @pl.when(is_owner)
    def _():
        for it in range(ITERS):
            wait_bytes(FB.at[it], sS.at[it])
        wait_bytes(FB.at[0, pl.ds(0, SLICES - 1)], sO)

    wait_bytes(out_ref, rO)


def vm(*shape):
    return pltpu.VMEM(shape, jnp.float32)


def per_device(initial, conductivity, source):
    dma = pltpu.SemaphoreType.DMA
    zl = (BY, NX)
    yl = (BZ, NX)
    return pl.pallas_call(
        kernel,
        out_shape=jax.ShapeDtypeStruct((1, SLAB, NY, NX), jnp.float32),
        in_specs=[pl.BlockSpec(memory_space=pl.ANY)] * 3,
        out_specs=pl.BlockSpec(memory_space=pl.ANY),
        scratch_shapes=[
            vm(BZ, WIN, NX), vm(BZ, BY, NX), vm(2, *zl), vm(BZ + 1, *zl), vm(BY + 1, *yl),
            vm(3, *zl), vm(NA, 3, *zl), vm(3, *yl), vm(NC, 3, *yl),
            vm(NA + 1, *zl), vm(NA, *zl), vm(NA, *zl), vm(NA, *zl),
            vm(NC + 1, *yl), vm(NC, *yl), vm(NC, *yl), vm(NC, *yl),
            vm(4, BZ, *zl), vm(4, BY, *yl), vm(2 * (NA - 1), *zl), vm(2 * (NC - 1), *yl),
            vm(2, 4, 16, 16, NX), vm(2, 14, 16, NX), vm(BZ * BY, NX),
            vm(3, 2, NY, NX), vm(2, NY, NX), vm(4, 16, 8, NX), vm(14, 8, NX),
            vm(4, 8, 16, NX), vm(14, 16, NX), vm(NX, 2 * NY), vm(2 * NY, NX),
            vm(ITERS, BZ, BY, NX), vm(ITERS, SLICES, 2, NY, NX), vm(ITERS + 1, SLICES + 1, 2, NY, NX),
            vm(STEPS, 2, *zl), vm(STEPS, NA - 1, *zl), vm(STEPS, 2, 8, NX), vm(STEPS, 2, 8, NX),
            dma((4,)), dma((3,)), dma((2,)), dma((2,)),
            dma((STEPS,)), dma((STEPS,)), dma((STEPS, 2)), dma((STEPS, 2)),
            dma((ITERS, SLICES)), dma((ITERS,)), dma((ITERS,)), dma((ITERS,)), dma, dma, dma((5,)),
            vm(SLAB, NY, NX), vm(SLAB, NY, NX),
        ],
        compiler_params=pltpu.CompilerParams(
            collective_id=0, has_side_effects=True, vmem_limit_bytes=60 * 1024 * 1024
        ),
        name="parareal",
    )(initial, conductivity, source)


def solution(mesh):
    placed = P("pencil", None, None)
    return jax.shard_map(
        per_device,
        mesh=mesh,
        in_specs=(placed, placed, placed),
        out_specs=P("tm", "pencil", None, None),
        check_vma=False,
    )
```

```python
import jax
import jax.numpy as jnp
from jax import lax
from jax.experimental import pallas as pl
from jax.experimental.pallas import tpu as pltpu
from jax.sharding import PartitionSpec as P

MESH = pl.DeviceIdType.MESH
FINE = 4
ITERS = 2
SLICES = 8
NA = 8
NB = 4
NC = 2
BZ = 16
BY = 32
SLAB = 4
NX = 128
NY = 64
WIN = BY + 8
STEPS = ITERS * FINE
FAR_FIRST = (4, 3, 5, 2, 6, 1, 7)
fine_dt = 0.5
coarse_dt = 2.0
vertical_ratio = 64.0


def harmonic(one, other):
    return 2.0 * one * other / (one + other)


def tree_sum(terms):
    terms = list(terms)
    while len(terms) > 1:
        terms = [
            terms[i] + terms[i + 1] if i + 1 < len(terms) else terms[i]
            for i in range(0, len(terms), 2)
        ]
    return terms[0]


def turn(values, amount):
    grouped = values.reshape(-1, 8, NX)
    return pltpu.roll(grouped, amount % 8, 1).reshape(values.shape)


def block_ends(faces, length):
    link = faces[0]
    ground_low = jnp.zeros_like(link)
    ground_high = jnp.ones_like(link)
    for i in range(1, length):
        face = faces[i]
        part = 1.0 / (link + ground_high + face)
        ground_low = ground_low + link * ground_high * part
        ground_high, link = (1.0 + face * ground_high * part, link * face * part)
    return ground_low, link, ground_high


def block_coefficients(faces, under, over, length, C):
    floor = faces[0]
    seen = 1.0 + floor * under / (floor + under)
    last = length - 1
    for i in range(last):
        face = faces[i + 1]
        inverse = 1.0 / (face + seen)
        C[1, i] = inverse
        C[0, i] = face * inverse
        seen = 1.0 + face * seen * inverse
    C[1, last] = 1.0 / (seen + over)
    part = jnp.ones_like(floor)
    C[3, last] = part
    for i in range(last - 1, -1, -1):
        part = part * C[0, i]
        C[3, i] = part
    seen = 1.0 + over
    steps = [None] * length
    for i in range(last - 1, -1, -1):
        face = faces[i + 1]
        inverse = 1.0 / (face + seen)
        steps[i + 1] = face * inverse
        seen = 1.0 + face * seen * inverse
    part = floor / (floor + seen)
    C[2, 0] = part
    for i in range(1, length):
        part = part * steps[i]
        C[2, i] = part
    C[0, last] = (floor + seen) / (seen * (floor + under) + floor * under)


def block_edges(rows, C):
    last = len(rows) - 1
    return (
        C[1, last] * tree_sum(C[3, i] * row for i, row in enumerate(rows)),
        C[0, last] * tree_sum(C[2, i] * row for i, row in enumerate(rows)),
    )


def block_inner(rows, C):
    last = len(rows) - 1
    swept = [rows[0]]
    for i in range(1, last + 1):
        swept.append(rows[i] + C[0, i - 1] * swept[i - 1])
    solved = [None] * (last + 1)
    solved[last] = C[1, last] * swept[last]
    for i in range(last - 1, -1, -1):
        solved[i] = C[1, i] * swept[i] + C[0, i] * solved[i + 1]
    return solved


def local_setup(kappas, factor, C, W):
    length = len(kappas)
    position = lax.broadcasted_iota(jnp.int32, kappas[0].shape, 0) % 8
    faces = [None] + [
        factor * harmonic(kappas[i], kappas[i + 1]) for i in range(length - 1)
    ]
    top = factor * harmonic(kappas[length - 1], turn(kappas[0], -1))
    faces[0] = turn(jnp.where(position == 7, 0.0, top), 1)
    ground_low, link, ground_high = block_ends(faces, length)
    down = jnp.ones_like(link)
    for _ in range(8):
        under = turn(down, 1)
        down_part = link / (link + ground_low + under)
        down = ground_high + down_part * (ground_low + under)
    under = turn(down, 1)
    up = jnp.zeros_like(link)
    for _ in range(8):
        over = jnp.where(position == 7, 0.0, turn(up, -1))
        up_part = link / (link + ground_high + over)
        up = ground_low + up_part * (ground_high + over)
    over = jnp.where(position == 7, 0.0, turn(up, -1))
    low_part = link / (link + ground_high + over)
    high_part = link / (link + ground_low + under)
    below = jnp.ones_like(link)
    above = jnp.ones_like(link)
    for k in range(1, 8):
        if k > 1:
            below = below * turn(low_part, k - 1)
            above = above * turn(high_part, 1 - k)
        W[k - 1] = jnp.where(position >= k, below, 0.0)
        W[7 + k - 1] = jnp.where(position + k < 8, above, 0.0)
    block_coefficients(faces, under, over, length, C)


def local_apply(rows, C, W):
    up, down = block_edges(rows, C)
    low = tree_sum(W[k - 1] * turn(up, k) for k in range(1, 8))
    high = tree_sum(W[7 + k - 1] * turn(down, -k) for k in range(1, 8))
    solved = block_inner(rows, C)
    return [
        value + C[2, i] * low + C[3, i] * high for i, value in enumerate(solved)
    ]


def kernel(
    init_ref, kap_ref, src_ref, out_ref,
    Kb, Sb, Kz, Gz, Gy, tz_s, tz_r, ty_s, ty_r,
    Ez, Lz, Uz, Mz, Ey, Ly, Uy, My, Cz, Cy, Wz, Wy, Cx, Wx, T,
    Ki, Hi, CXc, WXc, CYc, WYc, Tc, Lc,
    ST, FB, UB, mz_s, mz_r, my_s, my_r,
    r0, s0, r1, s1, rz, szm, ry, sym, rF, sF, rS, sS, rO, sO, rI, kap, src,
):
    t = lax.axis_index("tm")
    p = lax.axis_index("pencil")
    a = lax.div(p, NB)
    b = lax.rem(p, NB)
    y = lax.div(t, NC)
    half = lax.rem(t, NC)
    is_fine = lax.rem(b + y, 2) == 0
    odd = lax.rem(b + y, 2) == 1
    is_owner = jnp.logical_and(odd, half == 0)
    is_helper = jnp.logical_and(odd, half == 1)
    section = 2 * b + lax.div(y, 2)
    pair = lax.div(y, 2)
    owned = pl.ds(2 * pair, 2)

    def at_z(da):
        return (t, NB * lax.rem(a + da, NA) + b)

    def fine_device(n, h):
        bb = lax.div(n, 2)
        yy = lax.rem(bb, 2) + 2 * lax.rem(n, 2)
        return (NC * yy + h, NB * a + bb)

    def owner_device(bb, k):
        return (NC * (lax.rem(bb + 1, 2) + 2 * k), NB * a + bb)

    def send(src, dst, ssem, rsem, dev):
        pltpu.make_async_remote_copy(
            src_ref=src, dst_ref=dst, send_sem=ssem, recv_sem=rsem,
            device_id=dev, device_id_type=MESH,
        ).start()

    def wait_bytes(ref, sem):
        pltpu.make_async_copy(ref, ref, sem).wait()

    barrier = pltpu.get_barrier_semaphore()

    pltpu.make_async_copy(kap_ref, kap, rI.at[3]).start()
    pltpu.make_async_copy(src_ref, src, rI.at[4]).start()

    def greet(dev):
        pl.semaphore_signal(barrier, inc=1, device_id=dev, device_id_type=MESH)

    on_side = jnp.logical_or(b == 0, b == NB - 1)

    @pl.when(is_fine)
    def _():
        for i in FAR_FIRST:
            greet(at_z(i))

        @pl.when(b != NB - 1)
        def _():
            greet((t, NB * lax.rem(a + NA - 1, NA) + NB - 1))

        @pl.when(b != 0)
        def _():
            greet((t, NB * lax.rem(a + 1, NA)))

        greet((t, NB * a + lax.rem(b + 2, NB)))

        @pl.when(half == 1)
        def _():
            greet((t, NB * a + lax.rem(b + 1, NB)))
            greet((t, NB * a + lax.rem(b + 3, NB)))

        for i in (2, 1, 3, 0):
            for k in range(2):
                greet(owner_device(lax.rem(b + i, NB), k))
        greet((t + 1 - 2 * half, p))
        pl.semaphore_wait(barrier, (NA - 1) + 1 + 8 + 1 + jnp.where(on_side, 1, 0))

    @pl.when(is_owner)
    def _():
        def greet_slices(i, c):
            for h in range(NC):
                greet(fine_device(lax.rem(2 * b + 4 + i, SLICES), h))
            return c

        lax.fori_loop(0, SLICES, greet_slices, 0)
        greet(owner_device(b, 1 - pair))
        pltpu.make_async_copy(kap_ref.at[owned], Ki.at[0], rI.at[0]).start()
        pltpu.make_async_copy(src_ref.at[owned], Ki.at[1], rI.at[1]).start()
        pltpu.make_async_copy(init_ref.at[owned], Ki.at[2], rI.at[2]).start()
        pl.semaphore_wait(barrier, 16 + 3 + jnp.where(on_side, 2, 0))

    @pl.when(is_helper)
    def _():
        for k in range(2):
            greet(owner_device(b, k))
        pl.semaphore_wait(barrier, 2 + jnp.where(on_side, 2, 0))

    wait_bytes(kap, rI.at[3])
    first = pl.multiple_of(half * BY, 8)
    window = pl.ds(pl.multiple_of(half * (NY - WIN), 8), WIN)
    mine = pl.ds(SLAB * b, SLAB)
    even = lax.rem(y, 2)
    for i in range(2):
        target = even + 2 * i

        @pl.when(target != b)
        def _():
            send(kap.at[:, window, :], Kb.at[mine], s0.at[0], r0.at[0], (t, NB * a + target))

        @pl.when(target == b)
        def _():
            pltpu.make_async_copy(kap.at[:, window, :], Kb.at[mine], r0.at[0]).start()

    for side, layer, da in ((NB - 1, SLAB - 1, 1), (0, 0, NA - 1)):

        @pl.when(b == side)
        def _():
            for i in range(2):
                send(
                    kap.at[layer, pl.ds(first, BY), :],
                    Kz.at[0 if da == 1 else 1],
                    s0.at[2], r0.at[2 if da == 1 else 3],
                    (t, NB * lax.rem(a + da, NA) + even + 2 * i),
                )

    wait_bytes(src, rI.at[4])
    for i in range(2):
        target = even + 2 * i

        @pl.when(target != b)
        def _():
            send(src.at[:, pl.ds(first, BY), :], Sb.at[mine], s0.at[1], r0.at[1], (t, NB * a + target))

        @pl.when(target == b)
        def _():
            pltpu.make_async_copy(src.at[:, pl.ds(first, BY), :], Sb.at[mine], r0.at[1]).start()

    def give(it, n):
        for h in range(NC):
            send(
                UB.at[it, n, :, pl.ds(BY * h, BY), :],
                ST.at[it, pl.ds(SLAB * b + 2 * pair, 2)],
                sS.at[it], rS.at[it], fine_device(n, h),
            )

    def coarse(values):
        Tc[...] = values.reshape(2 * NY, NX).T
        rows = [Tc[pl.ds(i, 8, stride=16), :] for i in range(16)]
        for i, row in enumerate(local_apply(rows, CXc, WXc)):
            Tc[pl.ds(i, 8, stride=16), :] = row
        Lc[...] = Tc[...].T
        rows = [Lc[pl.ds(i, 16, stride=8), :] for i in range(8)]
        for i, row in enumerate(local_apply(rows, CYc, WYc)):
            Lc[pl.ds(i, 16, stride=8), :] = row
        return Lc[...].reshape(2, NY, NX)

    @pl.when(is_owner)
    def _():
        wait_bytes(Ki.at[0], rI.at[0])
        wait_bytes(Ki.at[1], rI.at[1])
        wait_bytes(Ki.at[2], rI.at[2])
        UB[0, 0] = Ki[2]
        UB[1, 0] = Ki[2]
        UB[2, 0] = Ki[2]
        give(0, 0)
        Lc[...] = Ki[0].reshape(2 * NY, NX)
        Tc[...] = Lc[...].T
        local_setup([Tc[pl.ds(i, 8, stride=16), :] for i in range(16)], coarse_dt, CXc, WXc)
        local_setup([Lc[pl.ds(i, 16, stride=8), :] for i in range(8)], coarse_dt, CYc, WYc)
        Hi[...] = coarse_dt * Ki[1]

        def advance(n, c):
            UB[0, n] = coarse(UB[0, n - 1] + Hi[...])
            give(0, n)
            return c

        lax.fori_loop(1, SLICES, advance, 0)
        UB[0, SLICES] = coarse(UB[0, SLICES - 1] + Hi[...])

    def split_setup(faces, tr, E, L, U, M, C, W, place, count, length):
        down = jnp.ones_like(faces[0])
        E[0] = down
        for j in range(count):
            ground_low, link, ground_high = tr[j, 0], tr[j, 1], tr[j, 2]
            passed = link / (link + ground_low + down)
            M[j] = passed
            down = ground_high + passed * (ground_low + down)
            E[j + 1] = down
        up = jnp.zeros_like(down)
        for j in range(count - 1, -1, -1):
            ground_low, link, ground_high = tr[j, 0], tr[j, 1], tr[j, 2]
            U[j] = up
            passed = link / (link + ground_high + up)
            L[j] = passed
            up = ground_low + passed * (ground_high + up)
        one = jnp.ones_like(down)
        below, above = [None], [None]
        part = one
        for i in range(1, count):
            if i > 1:
                part = part * L[lax.rem(place + count - i + 1, count)]
            below.append(jnp.where(place >= i, part, 0.0))
        part = one
        for i in range(1, count):
            if i > 1:
                part = part * M[lax.rem(place + i - 1, count)]
            above.append(jnp.where(place + i < count, part, 0.0))
        for i in range(1, count):
            W[i - 1] = below[count - i]
            W[count - 1 + i - 1] = above[i]
        block_coefficients(faces, E[place], U[place], length, C)

    def join(got, W):
        count = len(got)
        return (
            tree_sum(W[i] * got[i] for i in range(count)),
            tree_sum(W[count + i] * got[i] for i in range(count)),
        )

    @pl.when(is_fine)
    def _():
        wait_bytes(Kb, r0.at[0])
        wait_bytes(Kz.at[0], r0.at[2])
        wait_bytes(Kz.at[1], r0.at[3])
        row0 = 8 * half
        rows_of_k = Kb.reshape(BZ * WIN, NX)

        def kappa_z(z):
            return rows_of_k[pl.ds(pl.multiple_of(z * WIN + row0, 8), BY), :]

        def kappa_y(i):
            return rows_of_k[pl.ds(jnp.clip(row0 + i, 0, WIN - 1), BZ, stride=WIN), :]

        def outside(G, ts, first_k, inner, last_k, lowest, highest, factor, length):
            previous = first_k
            for i in range(length + 1):
                following = inner(i) if i < length else last_k
                face = factor * harmonic(previous, following)
                if i == 0:
                    face = jnp.where(lowest, 0.0, face)
                if i == length:
                    face = jnp.where(highest, 0.0, face)
                G[i] = face
                previous = following
            for i, part in enumerate(block_ends(G, length)):
                ts[i] = part

        outside(Gz, tz_s, Kz[0], kappa_z, Kz[1], a == 0, a == NA - 1, fine_dt * vertical_ratio, BZ)
        for i in FAR_FIRST:
            send(tz_s, tz_r.at[a], s1.at[0], r1.at[0], at_z(i))
        pltpu.make_async_copy(tz_s, tz_r.at[a], r1.at[0]).start()
        outside(Gy, ty_s, kappa_y(-1), kappa_y, kappa_y(BY), half == 0, half == 1, fine_dt, BY)
        partner = (t + 1 - 2 * half, p)
        send(ty_s, ty_r.at[half], s1.at[1], r1.at[1], partner)
        pltpu.make_async_copy(ty_s, ty_r.at[half], r1.at[1]).start()

        for z in range(BZ):
            T[pl.ds(BY * z, BY), :] = kappa_z(z)
        for tile in range(4):
            T[pl.ds(NX * tile, NX), :] = T[pl.ds(NX * tile, NX), :].T
        for g in range(2):
            local_setup(
                [T[pl.ds(2 * NX * g + i, 16, stride=16), :] for i in range(16)],
                fine_dt, Cx.at[g], Wx.at[g],
            )
        wait_bytes(ty_r, r1.at[1])
        split_setup(Gy, ty_r, Ey, Ly, Uy, My, Cy, Wy, half, NC, BY)
        wait_bytes(Sb, r0.at[1])
        for z in range(BZ):
            Sb[z] = fine_dt * Sb[z]

        def solve_xy(it, st):
            V = ST.at[it].reshape(BZ * BY, NX)
            kept = []
            for g in range(2):
                for tile in range(2 * g, 2 * g + 2):
                    start = V[pl.ds(NX * tile, NX), :] + Sb[4 * tile : 4 * tile + 4].reshape(NX, NX)
                    T[pl.ds(NX * tile, NX), :] = start.T
                rows = [T[pl.ds(2 * NX * g + i, 16, stride=16), :] for i in range(16)]
                for i, row in enumerate(local_apply(rows, Cx.at[g], Wx.at[g])):
                    T[pl.ds(2 * NX * g + i, 16, stride=16), :] = row
                for tile in range(2 * g, 2 * g + 2):
                    V[pl.ds(NX * tile, NX), :] = T[pl.ds(NX * tile, NX), :].T
                C = Cy.at[:, :, pl.ds(8 * g, 8), :]
                rows = [V[pl.ds(8 * BY * g + i, 8, stride=BY), :] for i in range(BY)]
                kept.append(rows)
                up, down = block_edges(rows, C)
                my_s[st, g] = jnp.where(half == 0, up, down)
                send(my_s.at[st, g], my_r.at[st, g], sym.at[st, g], ry.at[st, g], partner)
            for g in range(2):
                C = Cy.at[:, :, pl.ds(8 * g, 8), :]
                solved = block_inner(kept[g], C)
                wait_bytes(my_r.at[st, g], ry.at[st, g])
                got = my_r[st, g]
                low, high = (Wy[0, 8 * g : 8 * g + 8] * got, Wy[1, 8 * g : 8 * g + 8] * got)
                for i in range(BY):
                    V[pl.ds(8 * BY * g + i, 8, stride=BY), :] = (
                        solved[i] + C[2, i] * low + C[3, i] * high
                    )

        ring = [(i, at_z(i), jnp.where(a + i < NA, 0, 1)) for i in FAR_FIRST]

        def solve_z(it, st):
            V = ST.at[it].reshape(BZ * BY, NX)
            rows = [V[pl.ds(BY * i, BY), :] for i in range(BZ)]
            up, down = block_edges(rows, Cz)
            mz_s[st, 0] = up
            mz_s[st, 1] = down
            for i, device, which in ring:
                send(mz_s.at[st, which], mz_r.at[st, NA - 1 - i], szm.at[st], rz.at[st], device)
            solved = block_inner(rows, Cz)
            wait_bytes(mz_r.at[st], rz.at[st])
            low, high = join([mz_r[st, i] for i in range(NA - 1)], Wz)
            for i in range(BZ):
                V[pl.ds(BY * i, BY), :] = solved[i] + Cz[2, i] * low + Cz[3, i] * high

        for it in range(ITERS):
            wait_bytes(ST.at[it], rS.at[it])
            solve_xy(it, it * FINE)
            if it == 0:
                wait_bytes(tz_r, r1.at[0])
                split_setup(Gz, tz_r, Ez, Lz, Uz, Mz, Cz, Wz, a, NA, BZ)

            def one_step(s, c):
                solve_z(it, it * FINE + s)
                solve_xy(it, it * FINE + s + 1)
                return c

            lax.fori_loop(0, FINE - 1, one_step, 0)
            solve_z(it, it * FINE + FINE - 1)

            for i in (2, 1, 3, 0):
                bb = lax.rem(b + i, NB)
                for k in range(2):
                    send(
                        ST.at[it, pl.ds(SLAB * bb + 2 * k, 2)],
                        FB.at[it, section, :, pl.ds(first, BY), :],
                        sF.at[it], rF.at[it, section], owner_device(bb, k),
                    )

    @pl.when(is_owner)
    def _():
        for it in range(ITERS):
            last_turn = it == ITERS - 1

            def correct(n, before):
                wait_bytes(FB.at[it, n], rF.at[it, n])
                value = coarse(before) + (FB[it, n] - UB[it, n + 1])
                UB[it + 1, n + 1] = UB[it, n + 1] + value
                if last_turn:
                    done = UB.at[it + 1, n + 1]
                    dst = out_ref.at[0, owned]

                    @pl.when(n == t)
                    def _():
                        pltpu.make_async_copy(done, dst, rO).start()

                    @pl.when(n != t)
                    def _():
                        send(done, dst, sO, rO, (n, p))
                else:

                    @pl.when(n + 1 < SLICES)
                    def _():
                        give(it + 1, n + 1)
                return value

            if not last_turn:
                give(it + 1, 0)
            lax.fori_loop(0, SLICES, correct, jnp.zeros((2, NY, NX), jnp.float32))

    @pl.when(is_fine)
    def _():
        wait_bytes(Kb.at[pl.ds(0, SLAB)], s0.at[0])
        wait_bytes(Sb.at[pl.ds(0, SLAB)], s0.at[1])
        wait_bytes(tz_r.at[pl.ds(0, NA - 1)], s1.at[0])
        wait_bytes(ty_s, s1.at[1])

        def drain(st, c):
            wait_bytes(mz_r.at[st], szm.at[st])
            for g in range(2):
                wait_bytes(my_r.at[st, g], sym.at[st, g])
            return c

        lax.fori_loop(0, STEPS, drain, 0)
        for it in range(ITERS):
            wait_bytes(ST.at[it], sF.at[it])

    @pl.when(jnp.logical_or(b == 0, b == NB - 1))
    def _():
        wait_bytes(Kz, s0.at[2])

    @pl.when(odd)
    def _():
        wait_bytes(Kb.at[pl.ds(0, 2 * SLAB)], s0.at[0])
        wait_bytes(Sb.at[pl.ds(0, 2 * SLAB)], s0.at[1])

    @pl.when(is_owner)
    def _():
        for it in range(ITERS):
            wait_bytes(FB.at[it], sS.at[it])
        wait_bytes(FB.at[0, pl.ds(0, SLICES - 1)], sO)

    wait_bytes(out_ref, rO)


def vm(*shape):
    return pltpu.VMEM(shape, jnp.float32)


def per_device(initial, conductivity, source):
    dma = pltpu.SemaphoreType.DMA
    zl = (BY, NX)
    yl = (BZ, NX)
    return pl.pallas_call(
        kernel,
        out_shape=jax.ShapeDtypeStruct((1, SLAB, NY, NX), jnp.float32),
        in_specs=[pl.BlockSpec(memory_space=pl.ANY)] * 3,
        out_specs=pl.BlockSpec(memory_space=pl.ANY),
        scratch_shapes=[
            vm(BZ, WIN, NX), vm(BZ, BY, NX), vm(2, *zl), vm(BZ + 1, *zl), vm(BY + 1, *yl),
            vm(3, *zl), vm(NA, 3, *zl), vm(3, *yl), vm(NC, 3, *yl),
            vm(NA + 1, *zl), vm(NA, *zl), vm(NA, *zl), vm(NA, *zl),
            vm(NC + 1, *yl), vm(NC, *yl), vm(NC, *yl), vm(NC, *yl),
            vm(4, BZ, *zl), vm(4, BY, *yl), vm(2 * (NA - 1), *zl), vm(2 * (NC - 1), *yl),
            vm(2, 4, 16, 16, NX), vm(2, 14, 16, NX), vm(BZ * BY, NX),
            vm(3, 2, NY, NX), vm(2, NY, NX), vm(4, 16, 8, NX), vm(14, 8, NX),
            vm(4, 8, 16, NX), vm(14, 16, NX), vm(NX, 2 * NY), vm(2 * NY, NX),
            vm(ITERS, BZ, BY, NX), vm(ITERS, SLICES, 2, NY, NX), vm(ITERS + 1, SLICES + 1, 2, NY, NX),
            vm(STEPS, 2, *zl), vm(STEPS, NA - 1, *zl), vm(STEPS, 2, 8, NX), vm(STEPS, 2, 8, NX),
            dma((4,)), dma((3,)), dma((2,)), dma((2,)),
            dma((STEPS,)), dma((STEPS,)), dma((STEPS, 2)), dma((STEPS, 2)),
            dma((ITERS, SLICES)), dma((ITERS,)), dma((ITERS,)), dma((ITERS,)), dma, dma, dma((5,)),
            vm(SLAB, NY, NX), vm(SLAB, NY, NX),
        ],
        compiler_params=pltpu.CompilerParams(
            collective_id=0, has_side_effects=True, vmem_limit_bytes=60 * 1024 * 1024
        ),
        name="parareal",
    )(initial, conductivity, source)


def solution(mesh):
    placed = P("pencil", None, None)
    return jax.shard_map(
        per_device,
        mesh=mesh,
        in_specs=(placed, placed, placed),
        out_specs=P("tm", "pencil", None, None),
        check_vma=False,
    )
```

```python
import jax
import jax.numpy as jnp
from jax import lax
from jax.experimental import pallas as pl
from jax.experimental.pallas import tpu as pltpu
from jax.sharding import PartitionSpec as P

MESH = pl.DeviceIdType.MESH
FINE = 4
ITERS = 2
SLICES = 8
NA = 8
NB = 4
NC = 2
BZ = 16
BY = 32
SLAB = 4
NX = 128
NY = 64
WIN = BY + 8
STEPS = ITERS * FINE
FAR_FIRST = (4, 3, 5, 2, 6, 1, 7)
fine_dt = 0.5
coarse_dt = 2.0
vertical_ratio = 64.0


def harmonic(one, other):
    return 2.0 * one * other / (one + other)


def tree_sum(terms):
    terms = list(terms)
    while len(terms) > 1:
        terms = [
            terms[i] + terms[i + 1] if i + 1 < len(terms) else terms[i]
            for i in range(0, len(terms), 2)
        ]
    return terms[0]


def turn(values, amount):
    grouped = values.reshape(-1, 8, NX)
    return pltpu.roll(grouped, amount % 8, 1).reshape(values.shape)


def block_ends(faces, length):
    link = faces[0]
    ground_low = jnp.zeros_like(link)
    ground_high = jnp.ones_like(link)
    for i in range(1, length):
        face = faces[i]
        part = 1.0 / (link + ground_high + face)
        ground_low = ground_low + link * ground_high * part
        ground_high, link = (1.0 + face * ground_high * part, link * face * part)
    return ground_low, link, ground_high


def block_coefficients(faces, under, over, length, C):
    floor = faces[0]
    seen = 1.0 + floor * under / (floor + under)
    last = length - 1
    for i in range(last):
        face = faces[i + 1]
        inverse = 1.0 / (face + seen)
        C[1, i] = inverse
        C[0, i] = face * inverse
        seen = 1.0 + face * seen * inverse
    C[1, last] = 1.0 / (seen + over)
    part = jnp.ones_like(floor)
    C[3, last] = part
    for i in range(last - 1, -1, -1):
        part = part * C[0, i]
        C[3, i] = part
    seen = 1.0 + over
    steps = [None] * length
    for i in range(last - 1, -1, -1):
        face = faces[i + 1]
        inverse = 1.0 / (face + seen)
        steps[i + 1] = face * inverse
        seen = 1.0 + face * seen * inverse
    part = floor / (floor + seen)
    C[2, 0] = part
    for i in range(1, length):
        part = part * steps[i]
        C[2, i] = part
    C[0, last] = (floor + seen) / (seen * (floor + under) + floor * under)


def block_edges(rows, C):
    last = len(rows) - 1
    return (
        C[1, last] * tree_sum(C[3, i] * row for i, row in enumerate(rows)),
        C[0, last] * tree_sum(C[2, i] * row for i, row in enumerate(rows)),
    )


def block_inner(rows, C):
    last = len(rows) - 1
    swept = [rows[0]]
    for i in range(1, last + 1):
        swept.append(rows[i] + C[0, i - 1] * swept[i - 1])
    solved = [None] * (last + 1)
    solved[last] = C[1, last] * swept[last]
    for i in range(last - 1, -1, -1):
        solved[i] = C[1, i] * swept[i] + C[0, i] * solved[i + 1]
    return solved


def local_setup(kappas, factor, C, W):
    length = len(kappas)
    position = lax.broadcasted_iota(jnp.int32, kappas[0].shape, 0) % 8
    faces = [None] + [
        factor * harmonic(kappas[i], kappas[i + 1]) for i in range(length - 1)
    ]
    top = factor * harmonic(kappas[length - 1], turn(kappas[0], -1))
    faces[0] = turn(jnp.where(position == 7, 0.0, top), 1)
    ground_low, link, ground_high = block_ends(faces, length)
    down = jnp.ones_like(link)
    for _ in range(8):
        under = turn(down, 1)
        down_part = link / (link + ground_low + under)
        down = ground_high + down_part * (ground_low + under)
    under = turn(down, 1)
    up = jnp.zeros_like(link)
    for _ in range(8):
        over = jnp.where(position == 7, 0.0, turn(up, -1))
        up_part = link / (link + ground_high + over)
        up = ground_low + up_part * (ground_high + over)
    over = jnp.where(position == 7, 0.0, turn(up, -1))
    low_part = link / (link + ground_high + over)
    high_part = link / (link + ground_low + under)
    below = jnp.ones_like(link)
    above = jnp.ones_like(link)
    for k in range(1, 8):
        if k > 1:
            below = below * turn(low_part, k - 1)
            above = above * turn(high_part, 1 - k)
        W[k - 1] = jnp.where(position >= k, below, 0.0)
        W[7 + k - 1] = jnp.where(position + k < 8, above, 0.0)
    block_coefficients(faces, under, over, length, C)


def local_apply(rows, C, W):
    up, down = block_edges(rows, C)
    low = tree_sum(W[k - 1] * turn(up, k) for k in range(1, 8))
    high = tree_sum(W[7 + k - 1] * turn(down, -k) for k in range(1, 8))
    solved = block_inner(rows, C)
    return [
        value + C[2, i] * low + C[3, i] * high for i, value in enumerate(solved)
    ]


def kernel(
    init_ref, kap_ref, src_ref, out_ref,
    Kb, Sb, Kz, Gz, Gy, tz_s, tz_r, ty_s, ty_r,
    Ez, Lz, Uz, Mz, Ey, Ly, Uy, My, Cz, Cy, Wz, Wy, Cx, Wx, T,
    Ki, Hi, CXc, WXc, CYc, WYc, Tc, Lc,
    ST, FB, UB, mz_s, mz_r, my_s, my_r,
    r0, s0, r1, s1, rz, szm, ry, sym, rF, sF, rS, sS, rO, sO, rI, kap, src,
):
    t = lax.axis_index("tm")
    p = lax.axis_index("pencil")
    a = lax.div(p, NB)
    b = lax.rem(p, NB)
    y = lax.div(t, NC)
    half = lax.rem(t, NC)
    is_fine = lax.rem(b + y, 2) == 0
    odd = lax.rem(b + y, 2) == 1
    is_owner = jnp.logical_and(odd, half == 0)
    is_helper = jnp.logical_and(odd, half == 1)
    section = 2 * b + lax.div(y, 2)
    pair = lax.div(y, 2)
    owned = pl.ds(2 * pair, 2)

    def at_z(da):
        return (t, NB * lax.rem(a + da, NA) + b)

    def fine_device(n, h):
        bb = lax.div(n, 2)
        yy = lax.rem(bb, 2) + 2 * lax.rem(n, 2)
        return (NC * yy + h, NB * a + bb)

    def owner_device(bb, k):
        return (NC * (lax.rem(bb + 1, 2) + 2 * k), NB * a + bb)

    def send(src, dst, ssem, rsem, dev):
        pltpu.make_async_remote_copy(
            src_ref=src, dst_ref=dst, send_sem=ssem, recv_sem=rsem,
            device_id=dev, device_id_type=MESH,
        ).start()

    def wait_bytes(ref, sem):
        pltpu.make_async_copy(ref, ref, sem).wait()

    barrier = pltpu.get_barrier_semaphore()

    pltpu.make_async_copy(kap_ref, kap, rI.at[3]).start()
    pltpu.make_async_copy(src_ref, src, rI.at[4]).start()

    def greet(dev):
        pl.semaphore_signal(barrier, inc=1, device_id=dev, device_id_type=MESH)

    on_side = jnp.logical_or(b == 0, b == NB - 1)

    @pl.when(is_fine)
    def _():
        for i in FAR_FIRST:
            greet(at_z(i))

        @pl.when(b != NB - 1)
        def _():
            greet((t, NB * lax.rem(a + NA - 1, NA) + NB - 1))

        @pl.when(b != 0)
        def _():
            greet((t, NB * lax.rem(a + 1, NA)))

        greet((t, NB * a + lax.rem(b + 2, NB)))

        @pl.when(half == 1)
        def _():
            greet((t, NB * a + lax.rem(b + 1, NB)))
            greet((t, NB * a + lax.rem(b + 3, NB)))

        for i in (2, 1, 3, 0):
            for k in range(2):
                greet(owner_device(lax.rem(b + i, NB), k))
        greet((t + 1 - 2 * half, p))
        pl.semaphore_wait(barrier, (NA - 1) + 1 + 8 + 1 + jnp.where(on_side, 1, 0))

    @pl.when(is_owner)
    def _():
        def greet_slices(i, c):
            for h in range(NC):
                greet(fine_device(lax.rem(2 * b + 4 + i, SLICES), h))
            return c

        lax.fori_loop(0, SLICES, greet_slices, 0)
        greet(owner_device(b, 1 - pair))
        pltpu.make_async_copy(kap_ref.at[owned], Ki.at[0], rI.at[0]).start()
        pltpu.make_async_copy(src_ref.at[owned], Ki.at[1], rI.at[1]).start()
        pltpu.make_async_copy(init_ref.at[owned], Ki.at[2], rI.at[2]).start()
        pl.semaphore_wait(barrier, 16 + 3 + jnp.where(on_side, 2, 0))

    @pl.when(is_helper)
    def _():
        for k in range(2):
            greet(owner_device(b, k))
        pl.semaphore_wait(barrier, 2 + jnp.where(on_side, 2, 0))

    wait_bytes(kap, rI.at[3])
    first = pl.multiple_of(half * BY, 8)
    inside = pl.ds(pl.multiple_of(8 * half, 8), BY)
    beside = pl.ds(pl.multiple_of(BY - BY * half, 8), 8)
    beside_src = pl.ds(pl.multiple_of(BY - 8 * half, 8), 8)
    mine = pl.ds(SLAB * b, SLAB)
    even = lax.rem(y, 2)

    def spread(src_rows, dst_rows, ssem, rsem):
        for i in range(2):
            target = even + 2 * i
            here = kap.at[:, src_rows, :]
            there = Kb.at[mine, dst_rows, :]

            @pl.when(target != b)
            def _():
                send(here, there, ssem, rsem, (t, NB * a + target))

            @pl.when(target == b)
            def _():
                pltpu.make_async_copy(here, there, rsem).start()

    spread(pl.ds(first, BY), inside, s0.at[0], r0.at[0])
    for side, layer, da in ((NB - 1, SLAB - 1, 1), (0, 0, NA - 1)):

        @pl.when(b == side)
        def _():
            for i in range(2):
                send(
                    kap.at[layer, pl.ds(first, BY), :],
                    Kz.at[0 if da == 1 else 1],
                    s0.at[2], r0.at[2 if da == 1 else 3],
                    (t, NB * lax.rem(a + da, NA) + even + 2 * i),
                )

    spread(beside_src, beside, s0.at[3], r0.at[4])
    wait_bytes(src, rI.at[4])
    for i in range(2):
        target = even + 2 * i

        @pl.when(target != b)
        def _():
            send(src.at[:, pl.ds(first, BY), :], Sb.at[mine], s0.at[1], r0.at[1], (t, NB * a + target))

        @pl.when(target == b)
        def _():
            pltpu.make_async_copy(src.at[:, pl.ds(first, BY), :], Sb.at[mine], r0.at[1]).start()

    def give(it, n):
        for h in range(NC):
            send(
                UB.at[it, n, :, pl.ds(BY * h, BY), :],
                ST.at[it, pl.ds(SLAB * b + 2 * pair, 2)],
                sS.at[it], rS.at[it], fine_device(n, h),
            )

    def coarse(values):
        Tc[...] = values.reshape(2 * NY, NX).T
        rows = [Tc[pl.ds(i, 8, stride=16), :] for i in range(16)]
        for i, row in enumerate(local_apply(rows, CXc, WXc)):
            Tc[pl.ds(i, 8, stride=16), :] = row
        Lc[...] = Tc[...].T
        rows = [Lc[pl.ds(i, 16, stride=8), :] for i in range(8)]
        for i, row in enumerate(local_apply(rows, CYc, WYc)):
            Lc[pl.ds(i, 16, stride=8), :] = row
        return Lc[...].reshape(2, NY, NX)

    @pl.when(is_owner)
    def _():
        wait_bytes(Ki.at[0], rI.at[0])
        wait_bytes(Ki.at[1], rI.at[1])
        wait_bytes(Ki.at[2], rI.at[2])
        UB[0, 0] = Ki[2]
        UB[1, 0] = Ki[2]
        UB[2, 0] = Ki[2]
        give(0, 0)
        Lc[...] = Ki[0].reshape(2 * NY, NX)
        Tc[...] = Lc[...].T
        local_setup([Tc[pl.ds(i, 8, stride=16), :] for i in range(16)], coarse_dt, CXc, WXc)
        local_setup([Lc[pl.ds(i, 16, stride=8), :] for i in range(8)], coarse_dt, CYc, WYc)
        Hi[...] = coarse_dt * Ki[1]

        def advance(n, c):
            UB[0, n] = coarse(UB[0, n - 1] + Hi[...])
            give(0, n)
            return c

        lax.fori_loop(1, SLICES, advance, 0)
        UB[0, SLICES] = coarse(UB[0, SLICES - 1] + Hi[...])

    def split_setup(faces, tr, E, L, U, M, C, W, place, count, length):
        down = jnp.ones_like(faces[0])
        E[0] = down
        for j in range(count):
            ground_low, link, ground_high = tr[j, 0], tr[j, 1], tr[j, 2]
            passed = link / (link + ground_low + down)
            M[j] = passed
            down = ground_high + passed * (ground_low + down)
            E[j + 1] = down
        up = jnp.zeros_like(down)
        for j in range(count - 1, -1, -1):
            ground_low, link, ground_high = tr[j, 0], tr[j, 1], tr[j, 2]
            U[j] = up
            passed = link / (link + ground_high + up)
            L[j] = passed
            up = ground_low + passed * (ground_high + up)
        one = jnp.ones_like(down)
        below, above = [None], [None]
        part = one
        for i in range(1, count):
            if i > 1:
                part = part * L[lax.rem(place + count - i + 1, count)]
            below.append(jnp.where(place >= i, part, 0.0))
        part = one
        for i in range(1, count):
            if i > 1:
                part = part * M[lax.rem(place + i - 1, count)]
            above.append(jnp.where(place + i < count, part, 0.0))
        for i in range(1, count):
            W[i - 1] = below[count - i]
            W[count - 1 + i - 1] = above[i]
        block_coefficients(faces, E[place], U[place], length, C)

    def join(got, W):
        count = len(got)
        return (
            tree_sum(W[i] * got[i] for i in range(count)),
            tree_sum(W[count + i] * got[i] for i in range(count)),
        )

    @pl.when(is_fine)
    def _():
        wait_bytes(Kb.at[:, inside, :], r0.at[0])
        wait_bytes(Kz.at[0], r0.at[2])
        wait_bytes(Kz.at[1], r0.at[3])
        row0 = 8 * half
        rows_of_k = Kb.reshape(BZ * WIN, NX)

        def kappa_z(z):
            return rows_of_k[pl.ds(pl.multiple_of(z * WIN + row0, 8), BY), :]

        def kappa_y(i):
            return rows_of_k[pl.ds(jnp.clip(row0 + i, 0, WIN - 1), BZ, stride=WIN), :]

        def outside(G, ts, first_k, inner, last_k, lowest, highest, factor, length):
            previous = first_k
            for i in range(length + 1):
                following = inner(i) if i < length else last_k
                face = factor * harmonic(previous, following)
                if i == 0:
                    face = jnp.where(lowest, 0.0, face)
                if i == length:
                    face = jnp.where(highest, 0.0, face)
                G[i] = face
                previous = following
            for i, part in enumerate(block_ends(G, length)):
                ts[i] = part

        outside(Gz, tz_s, Kz[0], kappa_z, Kz[1], a == 0, a == NA - 1, fine_dt * vertical_ratio, BZ)
        for i in FAR_FIRST:
            send(tz_s, tz_r.at[a], s1.at[0], r1.at[0], at_z(i))
        pltpu.make_async_copy(tz_s, tz_r.at[a], r1.at[0]).start()
        wait_bytes(Kb.at[:, beside, :], r0.at[4])
        outside(Gy, ty_s, kappa_y(-1), kappa_y, kappa_y(BY), half == 0, half == 1, fine_dt, BY)
        partner = (t + 1 - 2 * half, p)
        send(ty_s, ty_r.at[half], s1.at[1], r1.at[1], partner)
        pltpu.make_async_copy(ty_s, ty_r.at[half], r1.at[1]).start()

        for z in range(BZ):
            T[pl.ds(BY * z, BY), :] = kappa_z(z)
        for tile in range(4):
            T[pl.ds(NX * tile, NX), :] = T[pl.ds(NX * tile, NX), :].T
        for g in range(2):
            local_setup(
                [T[pl.ds(2 * NX * g + i, 16, stride=16), :] for i in range(16)],
                fine_dt, Cx.at[g], Wx.at[g],
            )
        wait_bytes(ty_r, r1.at[1])
        split_setup(Gy, ty_r, Ey, Ly, Uy, My, Cy, Wy, half, NC, BY)
        wait_bytes(Sb, r0.at[1])
        for z in range(BZ):
            Sb[z] = fine_dt * Sb[z]

        def solve_xy(it, st):
            V = ST.at[it].reshape(BZ * BY, NX)
            kept = []
            for g in range(2):
                for tile in range(2 * g, 2 * g + 2):
                    start = V[pl.ds(NX * tile, NX), :] + Sb[4 * tile : 4 * tile + 4].reshape(NX, NX)
                    T[pl.ds(NX * tile, NX), :] = start.T
                rows = [T[pl.ds(2 * NX * g + i, 16, stride=16), :] for i in range(16)]
                for i, row in enumerate(local_apply(rows, Cx.at[g], Wx.at[g])):
                    T[pl.ds(2 * NX * g + i, 16, stride=16), :] = row
                for tile in range(2 * g, 2 * g + 2):
                    V[pl.ds(NX * tile, NX), :] = T[pl.ds(NX * tile, NX), :].T
                C = Cy.at[:, :, pl.ds(8 * g, 8), :]
                rows = [V[pl.ds(8 * BY * g + i, 8, stride=BY), :] for i in range(BY)]
                kept.append(rows)
                up, down = block_edges(rows, C)
                my_s[st, g] = jnp.where(half == 0, up, down)
                send(my_s.at[st, g], my_r.at[st, g], sym.at[st, g], ry.at[st, g], partner)
            for g in range(2):
                C = Cy.at[:, :, pl.ds(8 * g, 8), :]
                solved = block_inner(kept[g], C)
                wait_bytes(my_r.at[st, g], ry.at[st, g])
                got = my_r[st, g]
                low, high = (Wy[0, 8 * g : 8 * g + 8] * got, Wy[1, 8 * g : 8 * g + 8] * got)
                for i in range(BY):
                    V[pl.ds(8 * BY * g + i, 8, stride=BY), :] = (
                        solved[i] + C[2, i] * low + C[3, i] * high
                    )

        ring = [(i, at_z(i), jnp.where(a + i < NA, 0, 1)) for i in FAR_FIRST]

        def solve_z(it, st):
            V = ST.at[it].reshape(BZ * BY, NX)
            rows = [V[pl.ds(BY * i, BY), :] for i in range(BZ)]
            up, down = block_edges(rows, Cz)
            mz_s[st, 0] = up
            mz_s[st, 1] = down
            for i, device, which in ring:
                send(mz_s.at[st, which], mz_r.at[st, NA - 1 - i], szm.at[st], rz.at[st], device)
            solved = block_inner(rows, Cz)
            wait_bytes(mz_r.at[st], rz.at[st])
            low, high = join([mz_r[st, i] for i in range(NA - 1)], Wz)
            for i in range(BZ):
                V[pl.ds(BY * i, BY), :] = solved[i] + Cz[2, i] * low + Cz[3, i] * high

        for it in range(ITERS):
            wait_bytes(ST.at[it], rS.at[it])
            solve_xy(it, it * FINE)
            if it == 0:
                wait_bytes(tz_r, r1.at[0])
                split_setup(Gz, tz_r, Ez, Lz, Uz, Mz, Cz, Wz, a, NA, BZ)

            def one_step(s, c):
                solve_z(it, it * FINE + s)
                solve_xy(it, it * FINE + s + 1)
                return c

            lax.fori_loop(0, FINE - 1, one_step, 0)
            solve_z(it, it * FINE + FINE - 1)

            for i in (2, 1, 3, 0):
                bb = lax.rem(b + i, NB)
                for k in range(2):
                    send(
                        ST.at[it, pl.ds(SLAB * bb + 2 * k, 2)],
                        FB.at[it, section, :, pl.ds(first, BY), :],
                        sF.at[it], rF.at[it, section], owner_device(bb, k),
                    )

    @pl.when(is_owner)
    def _():
        for it in range(ITERS):
            last_turn = it == ITERS - 1

            def correct(n, before):
                wait_bytes(FB.at[it, n], rF.at[it, n])
                value = coarse(before) + (FB[it, n] - UB[it, n + 1])
                UB[it + 1, n + 1] = UB[it, n + 1] + value
                if last_turn:
                    done = UB.at[it + 1, n + 1]
                    dst = out_ref.at[0, owned]

                    @pl.when(n == t)
                    def _():
                        pltpu.make_async_copy(done, dst, rO).start()

                    @pl.when(n != t)
                    def _():
                        send(done, dst, sO, rO, (n, p))
                else:

                    @pl.when(n + 1 < SLICES)
                    def _():
                        give(it + 1, n + 1)
                return value

            if not last_turn:
                give(it + 1, 0)
            lax.fori_loop(0, SLICES, correct, jnp.zeros((2, NY, NX), jnp.float32))

    @pl.when(is_fine)
    def _():
        wait_bytes(Kb.at[pl.ds(0, SLAB), inside, :], s0.at[0])
        wait_bytes(Kb.at[pl.ds(0, SLAB), beside, :], s0.at[3])
        wait_bytes(Sb.at[pl.ds(0, SLAB)], s0.at[1])
        wait_bytes(tz_r.at[pl.ds(0, NA - 1)], s1.at[0])
        wait_bytes(ty_s, s1.at[1])

        def drain(st, c):
            wait_bytes(mz_r.at[st], szm.at[st])
            for g in range(2):
                wait_bytes(my_r.at[st, g], sym.at[st, g])
            return c

        lax.fori_loop(0, STEPS, drain, 0)
        for it in range(ITERS):
            wait_bytes(ST.at[it], sF.at[it])

    @pl.when(jnp.logical_or(b == 0, b == NB - 1))
    def _():
        wait_bytes(Kz, s0.at[2])

    @pl.when(odd)
    def _():
        wait_bytes(Kb.at[pl.ds(0, 2 * SLAB), inside, :], s0.at[0])
        wait_bytes(Kb.at[pl.ds(0, 2 * SLAB), beside, :], s0.at[3])
        wait_bytes(Sb.at[pl.ds(0, 2 * SLAB)], s0.at[1])

    @pl.when(is_owner)
    def _():
        for it in range(ITERS):
            wait_bytes(FB.at[it], sS.at[it])
        wait_bytes(FB.at[0, pl.ds(0, SLICES - 1)], sO)

    wait_bytes(out_ref, rO)


def vm(*shape):
    return pltpu.VMEM(shape, jnp.float32)


def per_device(initial, conductivity, source):
    dma = pltpu.SemaphoreType.DMA
    zl = (BY, NX)
    yl = (BZ, NX)
    return pl.pallas_call(
        kernel,
        out_shape=jax.ShapeDtypeStruct((1, SLAB, NY, NX), jnp.float32),
        in_specs=[pl.BlockSpec(memory_space=pl.ANY)] * 3,
        out_specs=pl.BlockSpec(memory_space=pl.ANY),
        scratch_shapes=[
            vm(BZ, WIN, NX), vm(BZ, BY, NX), vm(2, *zl), vm(BZ + 1, *zl), vm(BY + 1, *yl),
            vm(3, *zl), vm(NA, 3, *zl), vm(3, *yl), vm(NC, 3, *yl),
            vm(NA + 1, *zl), vm(NA, *zl), vm(NA, *zl), vm(NA, *zl),
            vm(NC + 1, *yl), vm(NC, *yl), vm(NC, *yl), vm(NC, *yl),
            vm(4, BZ, *zl), vm(4, BY, *yl), vm(2 * (NA - 1), *zl), vm(2 * (NC - 1), *yl),
            vm(2, 4, 16, 16, NX), vm(2, 14, 16, NX), vm(BZ * BY, NX),
            vm(3, 2, NY, NX), vm(2, NY, NX), vm(4, 16, 8, NX), vm(14, 8, NX),
            vm(4, 8, 16, NX), vm(14, 16, NX), vm(NX, 2 * NY), vm(2 * NY, NX),
            vm(ITERS, BZ, BY, NX), vm(ITERS, SLICES, 2, NY, NX), vm(ITERS + 1, SLICES + 1, 2, NY, NX),
            vm(STEPS, 2, *zl), vm(STEPS, NA - 1, *zl), vm(STEPS, 2, 8, NX), vm(STEPS, 2, 8, NX),
            dma((5,)), dma((4,)), dma((2,)), dma((2,)),
            dma((STEPS,)), dma((STEPS,)), dma((STEPS, 2)), dma((STEPS, 2)),
            dma((ITERS, SLICES)), dma((ITERS,)), dma((ITERS,)), dma((ITERS,)), dma, dma, dma((5,)),
            vm(SLAB, NY, NX), vm(SLAB, NY, NX),
        ],
        compiler_params=pltpu.CompilerParams(
            collective_id=0, has_side_effects=True, vmem_limit_bytes=60 * 1024 * 1024
        ),
        name="parareal",
    )(initial, conductivity, source)


def solution(mesh):
    placed = P("pencil", None, None)
    return jax.shard_map(
        per_device,
        mesh=mesh,
        in_specs=(placed, placed, placed),
        out_specs=P("tm", "pencil", None, None),
        check_vma=False,
    )
```
